512 devices in a mesh: dom: 128 (over z, y, core), slab: 4 (over x).
Axes of the slice: x: 4, y: 4, z: 16, core: 2. Of those that a mesh axis runs over, the one named last changes fastest.
Arguments:
- features: bfloat16 [65536, 128], P(('dom', 'slab')), may hold values from -6 to 6
- positions: float32 [3, 65536], P(None, ('dom', 'slab')), may hold values from 0 to 4
- neighbours: int32 [32, 65536], P(None, ('dom', 'slab')), may hold values from 0 to 415, as said below
- neighbour_mask: int32 [32, 65536], P(None, ('dom', 'slab')), may hold values from 0 to 1
- ghost_list: int32 [16384], P(('dom', 'slab')), may hold values from 0 to 127, as said below
- w_up: bfloat16 [128, 128], replicated, may hold values from -0.5 to 0.5
- radial_weight_1: bfloat16 [8, 64], replicated, may hold values from -2 to 2
- radial_weight_2: bfloat16 [64, 64], replicated, may hold values from -0.75 to 0.75
- radial_weight_3: bfloat16 [64, 256], replicated, may hold values from -0.75 to 0.75
- w_a: bfloat16 [128, 128], replicated, may hold values from -0.5 to 0.5
- w_b: bfloat16 [128, 128], replicated, may hold values from -0.5 to 0.5
- w_o1: bfloat16 [128, 16], replicated, may hold values from -0.5 to 0.5
- w_o2: float32 [16], replicated, may hold values from -1.5 to 1.5
Outputs:
- energies: float32 [65536], P(('dom', 'slab'))
- forces: float32 [3, 65536], P(None, ('dom', 'slab'))
The draws below stay inside these ranges and needn't reach their ends.
Inputs may be any that keep to these rules, and one draw needn't show every extreme that they name: `neighbours`: A value below 128 is a local atom other than the slot's own atom; a larger value is 128 + b * 32 + r with block b in 0 .. 8 but never 4. `ghost_list`: the 32 entries of each domain are distinct.
All inputs are finite; a program needn't handle non-finite values.
Results may differ from the reference program's by a relative error of at most 0.015.
Values may be sent and summed in bfloat16 or wider, within the bound.
A program may use at most 64 MiB of HBM per device.

```python
import jax
import jax.numpy as jnp
from jax import lax

CHAN = 128
RADIAL = 64
BASIS = 8
READOUT = 16
NEIGH = 32
DOMAIN_ATOMS = 128
GHOST_DEV = 32
ATOMS = 65536
GHOSTS = 16384
EXTENDED = 416
N_DOM = 128
N_SLAB = 4


def draw_neighbours(key, part):
    key = jax.random.fold_in(key, 11)
    first, second, third, fourth = jax.random.split(key, 4)
    local = jnp.arange(ATOMS, dtype=jnp.int32) % DOMAIN_ATOMS
    stride = jax.random.randint(first, (NEIGH, ATOMS), 1, DOMAIN_ATOMS, dtype=jnp.int32)
    nearby = (local[None, :] + stride) % DOMAIN_ATOMS
    blocks = jax.random.randint(second, (NEIGH, ATOMS), 0, 8, dtype=jnp.int32)
    blocks = blocks + (blocks >= 4).astype(jnp.int32)
    remote = DOMAIN_ATOMS + blocks * GHOST_DEV + jax.random.randint(third, (NEIGH, ATOMS), 0, GHOST_DEV, dtype=jnp.int32)
    chosen = jax.random.randint(fourth, (NEIGH, ATOMS), 0, 5, dtype=jnp.int32) < 2
    return jnp.where(chosen, remote, nearby).astype(jnp.int32)


def draw_neighbour_mask(key, part):
    key = jax.random.fold_in(key, 12)
    first, second = jax.random.split(key, 2)
    domains = ATOMS // DOMAIN_ATOMS
    levels = jax.random.randint(first, (domains,), 1, 5, dtype=jnp.int32)
    atom_level = levels[jnp.arange(ATOMS, dtype=jnp.int32) // DOMAIN_ATOMS]
    coins = jax.random.randint(second, (NEIGH, ATOMS), 0, 4, dtype=jnp.int32)
    return (coins < atom_level[None, :]).astype(jnp.int32)


def draw_ghost_list(key, part):
    key = jax.random.fold_in(key, 13)
    domains = GHOSTS // GHOST_DEV
    keys = jax.random.split(key, domains)
    orders = jax.vmap(lambda single: jax.random.permutation(single, DOMAIN_ATOMS))(keys)
    return orders[:, :GHOST_DEV].reshape(-1).astype(jnp.int32)


def block_scale(own_key, shape, cuts, low, largest):
    def one(position, parts):
        draws = jax.random.uniform(jax.random.fold_in(jax.random.fold_in(own_key, 6), position), (parts,), jnp.float32, low / len(cuts), largest / len(cuts))
        return jnp.repeat(jnp.exp(draws), shape[position] // parts).reshape((-1,) + (1,) * (len(shape) - position - 1))

    level = one(*cuts[0])
    for cut in cuts[1:]:
        level = level * one(*cut)
    return level


def normal_values(stream_key, extent, scale, most, cuts=(), kind=jnp.bfloat16):
    loudness = block_scale(stream_key, extent, cuts, -0.22, 0.18) if cuts else 1.0
    entries = jax.random.normal(stream_key, extent, jnp.float32) * scale * loudness
    return jnp.minimum(jnp.maximum(entries, -most), most).astype(kind)


def setup_inputs(seed: int = 0) -> dict:
    key_list = jax.random.split(jax.random.key(seed), 14)
    features = normal_values(key_list[0], (ATOMS, CHAN), 1.0, 6.0, ((0, 512),))
    positions = jnp.clip(4.0 * jax.random.uniform(key_list[1], (3, ATOMS), jnp.float32) ** block_scale(key_list[1], (3, ATOMS), ((1, 512),), -0.2, 0.2), 0.0, 4.0)
    neighbours = draw_neighbours(jax.random.fold_in(key_list[13], 71), 0)
    neighbour_mask = draw_neighbour_mask(jax.random.fold_in(key_list[13], 71), 0)
    ghost_list = draw_ghost_list(jax.random.fold_in(key_list[13], 71), 0)
    w_up = normal_values(key_list[5], (CHAN, CHAN), CHAN ** -0.5, 0.5)
    radial_weight_1 = normal_values(key_list[6], (BASIS, RADIAL), BASIS ** -0.5, 2.0)
    radial_weight_2 = normal_values(key_list[7], (RADIAL, RADIAL), RADIAL ** -0.5, 0.75)
    radial_weight_3 = normal_values(key_list[8], (RADIAL, 2 * CHAN), RADIAL ** -0.5, 0.75)
    w_a = normal_values(key_list[9], (CHAN, CHAN), CHAN ** -0.5, 0.5)
    w_b = normal_values(key_list[10], (CHAN, CHAN), CHAN ** -0.5, 0.5)
    w_o1 = normal_values(key_list[11], (CHAN, READOUT), CHAN ** -0.5, 0.5)
    w_o2 = normal_values(key_list[12], (READOUT,), READOUT ** -0.5, 1.5, (), jnp.float32)
    return dict(features=features, positions=positions, neighbours=neighbours, neighbour_mask=neighbour_mask, ghost_list=ghost_list, w_up=w_up, radial_weight_1=radial_weight_1, radial_weight_2=radial_weight_2, radial_weight_3=radial_weight_3, w_a=w_a, w_b=w_b, w_o1=w_o1, w_o2=w_o2)


pairwise_scale = 1.0 / 16.0
cell_width = 4.0

def pair_messages(atom_coords, neighbour_coords, atom_projection, neighbour_projection, alive_flags, radial_weight_1, radial_weight_2, radial_weight_3):
    offset = neighbour_coords - atom_coords
    spread = jnp.sqrt(lax.optimization_barrier(jnp.sum(offset * offset, axis=0)) + 1.0)
    centers = 1.0 + 0.75 * jnp.arange(radial_weight_1.shape[0], dtype=jnp.float32)
    basis = jnp.exp(-jnp.square(spread[:, None] - centers[None, :])).astype(jnp.bfloat16)
    layer_one = jax.nn.silu(jnp.dot(basis, radial_weight_1, preferred_element_type=jnp.float32)).astype(jnp.bfloat16)
    second_layer = jax.nn.silu(jnp.dot(layer_one, radial_weight_2, preferred_element_type=jnp.float32)).astype(jnp.bfloat16)
    radial_filter = jnp.dot(second_layer, radial_weight_3, preferred_element_type=jnp.float32) * (alive_flags * pairwise_scale)[:, None]
    channels = atom_projection.shape[1]
    scalar_weight = radial_filter[:, :channels]
    vector_weight = radial_filter[:, channels:]
    direction = offset / spread[None, :]
    partner_wide = neighbour_projection.astype(jnp.float32)
    atom_wide = atom_projection.astype(jnp.float32)
    atom_scalar_message = scalar_weight * partner_wide
    atom_vector_message = direction[:, :, None] * (vector_weight * partner_wide)[None]
    neighbour_scalar_message = scalar_weight * atom_wide
    neighbour_vector_message = -direction[:, :, None] * (vector_weight * atom_wide)[None]
    return (atom_scalar_message, atom_vector_message, neighbour_scalar_message, neighbour_vector_message)

def node_energy(agg_s, agg_v, features, w_a, w_b, w_o1, w_o2):
    norms = lax.optimization_barrier(jnp.sum(agg_v * agg_v, axis=0))
    mixed = features.astype(jnp.float32) + jnp.dot(agg_s.astype(jnp.bfloat16), w_a, preferred_element_type=jnp.float32)
    mixed = mixed + jnp.dot(norms.astype(jnp.bfloat16), w_b, preferred_element_type=jnp.float32)
    hidden = jax.nn.silu(jnp.dot(mixed.astype(jnp.bfloat16), w_o1, preferred_element_type=jnp.float32))
    return lax.optimization_barrier(jnp.sum(hidden * w_o2[None, :], axis=1))

def extended_rows(ghost_list, domains):
    owner = jnp.arange(domains, dtype=jnp.int32)
    row_dom = owner // N_SLAB
    row_slab = owner % N_SLAB
    lists = ghost_list.reshape(domains, GHOST_DEV)
    pieces = [owner[:, None] * DOMAIN_ATOMS + jnp.arange(DOMAIN_ATOMS, dtype=jnp.int32)[None, :]]
    shift_first = [jnp.zeros((DOMAIN_ATOMS,), jnp.float32)]
    shift_second = [jnp.zeros((DOMAIN_ATOMS,), jnp.float32)]
    for across in range(3):
        for along in range(3):
            source = (row_dom + across - 1) % N_DOM * N_SLAB + (row_slab + along - 1) % N_SLAB
            pieces.append(lists[source] + source[:, None] * DOMAIN_ATOMS)
            shift_first.append(jnp.full((GHOST_DEV,), (across - 1) * cell_width, jnp.float32))
            shift_second.append(jnp.full((GHOST_DEV,), (along - 1) * cell_width, jnp.float32))
    ext_ids = jnp.concatenate(pieces, axis=1).astype(jnp.int32)
    shifts = jnp.stack([jnp.concatenate(shift_first), jnp.concatenate(shift_second), jnp.zeros((EXTENDED,), jnp.float32)])
    return (ext_ids, shifts)

def reference(features, positions, neighbours, neighbour_mask, ghost_list, w_up, radial_weight_1, radial_weight_2, radial_weight_3, w_a, w_b, w_o1, w_o2):
    domains = N_DOM * N_SLAB
    proj = jnp.dot(features, w_up, preferred_element_type=jnp.float32).astype(jnp.bfloat16)
    ext_ids, shifts = extended_rows(ghost_list, domains)
    domain_rows = jnp.broadcast_to(jnp.arange(DOMAIN_ATOMS, dtype=jnp.int32)[None, :], (NEIGH, DOMAIN_ATOMS)).reshape(-1)

    def domain_payload(domain_index):
        row_numbers = ext_ids[domain_index]
        extended_coords = positions[:, row_numbers] + shifts
        extended_projection = proj[row_numbers]
        start_offset = (domain_index * DOMAIN_ATOMS).astype(jnp.int32)
        neighbour_table = lax.dynamic_slice_in_dim(neighbours, start_offset, DOMAIN_ATOMS, 1).reshape(-1)
        alive_flags = (lax.dynamic_slice_in_dim(neighbour_mask, start_offset, DOMAIN_ATOMS, 1) != 0).astype(jnp.float32).reshape(-1)
        return (row_numbers, extended_coords, extended_projection, neighbour_table, alive_flags)

    def forward_step(carry, domain_index):
        agg_s, agg_v = carry
        row_numbers, extended_coords, extended_projection, neighbour_table, alive_flags = domain_payload(domain_index)
        atom_scalar_message, atom_vector_message, neighbour_scalar_message, neighbour_vector_message = pair_messages(extended_coords[:, domain_rows], extended_coords[:, neighbour_table], extended_projection[domain_rows], extended_projection[neighbour_table], alive_flags, radial_weight_1, radial_weight_2, radial_weight_3)
        atom_ids = row_numbers[domain_rows]
        partner_ids = row_numbers[neighbour_table]
        agg_s = agg_s.at[atom_ids].add(atom_scalar_message).at[partner_ids].add(neighbour_scalar_message)
        agg_v = agg_v.at[:, atom_ids].add(atom_vector_message).at[:, partner_ids].add(neighbour_vector_message)
        return ((agg_s, agg_v), None)
    start_s = jnp.zeros((ATOMS, CHAN), jnp.float32)
    start_v = jnp.zeros((3, ATOMS, CHAN), jnp.float32)
    domain_ids = jnp.arange(domains, dtype=jnp.int32)
    (agg_s, agg_v), unused = lax.scan(forward_step, (start_s, start_v), domain_ids)

    def energy_of(summed, vectors):
        return node_energy(summed, vectors, features, w_a, w_b, w_o1, w_o2)
    energies, pull_nodes = jax.vjp(energy_of, agg_s, agg_v)
    cot_s, cot_v = pull_nodes(jnp.ones_like(energies))

    def backward_step(grad, domain_index):
        row_numbers, extended_coords, extended_projection, neighbour_table, alive_flags = domain_payload(domain_index)

        def positional(atom_endpoint, neighbour_endpoint):
            return pair_messages(atom_endpoint, neighbour_endpoint, extended_projection[domain_rows], extended_projection[neighbour_table], alive_flags, radial_weight_1, radial_weight_2, radial_weight_3)
        ignored, pull_edges = jax.vjp(positional, extended_coords[:, domain_rows], extended_coords[:, neighbour_table])
        atom_ids = row_numbers[domain_rows]
        partner_ids = row_numbers[neighbour_table]
        atom_grad, partner_grad = pull_edges((cot_s[atom_ids], cot_v[:, atom_ids], cot_s[partner_ids], cot_v[:, partner_ids]))
        grad = grad.at[:, atom_ids].add(atom_grad).at[:, partner_ids].add(partner_grad)
        return (grad, None)
    grad, unused = lax.scan(backward_step, jnp.zeros((3, ATOMS), jnp.float32), domain_ids)
    return (energies, -grad)
```

```python
import functools

import jax
import jax.numpy as jnp
from jax import lax
from jax.experimental import pallas as pl
from jax.experimental.pallas import tpu as pltpu
from jax.sharding import PartitionSpec as P

MESH = pl.DeviceIdType.MESH
F32 = jnp.float32
LOW = jnp.bfloat16
ATOMS = 128
CHAN = 128
LIST = 32
SLOTS = 32
HIDDEN = 64
GHOST = 8 * LIST
ROWS = ATOMS + GHOST
EDGES = SLOTS * ATOMS
PER = 4
CHUNK = PER * ATOMS
BANDS = 4
BAND = CHAN // BANDS
SIDES = [(a, b) for a in (-1, 0, 1) for b in (-1, 0, 1) if (a, b) != (0, 0)]
NN = (((1,), (0,)), ((), ()))
NT = (((1,), (1,)), ((), ()))


def dot(a, b, dims=NN):
    return lax.dot_general(a, b, dims, preferred_element_type=F32)


def sigmoid(x):
    return 0.5 * jnp.tanh(0.5 * x) + 0.5


def column(row, n):
    down = lax.broadcasted_iota(jnp.int32, (n, n), 0)
    across = lax.broadcasted_iota(jnp.int32, (n, n), 1)
    return jnp.sum(jnp.where(down == across, row, 0.0), axis=1, keepdims=True)


def split(x):
    high = x.astype(LOW)
    return high, (x - high.astype(F32)).astype(LOW)


def lanes_of(c):
    return pl.ds(pl.multiple_of(c * CHUNK, CHUNK), CHUNK)


def kernel(
    n_dom,
    n_slab,
    features_hbm,
    positions_hbm,
    neighbours_hbm,
    mask_hbm,
    list_hbm,
    w_up_hbm,
    w1_hbm,
    w2_hbm,
    w3_hbm,
    w_a_hbm,
    w_b_hbm,
    w_o1_hbm,
    w_o2_hbm,
    energies_ref,
    forces_ref,
    features,
    positions,
    neighbours,
    mask,
    ghost_list,
    w_up,
    w1,
    w2,
    w3,
    w_a,
    w_b,
    w_o1,
    w_o2,
    ext,
    ext_t,
    own_pos,
    pick,
    alive,
    hot,
    w1_t,
    w2_t,
    w3_t,
    w_a_t,
    w_b_t,
    w_o1_t,
    features_t,
    proj_t,
    partner,
    unit,
    inverse,
    slope,
    gate1,
    gate2,
    radial,
    messages,
    agg,
    cot,
    cot_ext,
    partner_cot,
    d_radial,
    d_unit,
    d_rel,
    send1,
    send2,
    recv2,
    send3,
    recv3,
    send4,
    recv4,
    load_sem,
    out_sem,
    in_sem,
):
    dom = lax.axis_index("dom")
    slab = lax.axis_index("slab")
    peers = [
        (lax.rem(dom + a + n_dom, n_dom), lax.rem(slab + b + n_slab, n_slab)) for a, b in SIDES
    ]
    barrier = pltpu.get_barrier_semaphore()
    for peer in peers:
        pl.semaphore_signal(barrier, inc=1, device_id=peer, device_id_type=MESH)

    def push(phase, j, src, dst):
        return pltpu.make_async_remote_copy(
            src_ref=src,
            dst_ref=dst,
            send_sem=out_sem.at[phase, j],
            recv_sem=in_sem.at[phase, 7 - j],
            device_id=peers[j],
            device_id_type=MESH,
        )

    pairs = [
        (features_hbm, features),
        (w_up_hbm, w_up),
        (positions_hbm, positions),
        (list_hbm, ghost_list),
        (neighbours_hbm, neighbours),
        (mask_hbm, mask),
        (w1_hbm, w1),
        (w2_hbm, w2),
        (w3_hbm, w3),
        (w_a_hbm, w_a),
        (w_b_hbm, w_b),
        (w_o1_hbm, w_o1),
        (w_o2_hbm, w_o2),
    ]
    loads = [pltpu.make_async_copy(a, b, load_sem.at[i]) for i, (a, b) in enumerate(pairs)]
    for load in loads:
        load.start()
    for load in loads[:4]:
        load.wait()

    proj = dot(features[...], w_up[...]).astype(LOW)
    own_pos[...] = jnp.zeros_like(own_pos)
    own_pos[0:3, :] = positions[...]
    coords = own_pos[...]
    high = coords.astype(LOW).astype(F32)
    rest = coords - high
    middle = rest.astype(LOW).astype(F32)
    pieces = jnp.concatenate(
        [high, middle, rest - middle, jnp.zeros((CHAN - 24, ATOMS), F32)], axis=0
    )
    ext[0:ATOMS, 0:CHAN] = proj
    ext[0:ATOMS, CHAN : 2 * CHAN] = pieces.T.astype(LOW)
    list_column = column(ghost_list[...].astype(F32), LIST)
    atom_lane = lax.broadcasted_iota(jnp.int32, (LIST, ATOMS), 1).astype(F32)
    pick[...] = jnp.where(atom_lane == list_column, 1.0, 0.0).astype(LOW)
    send1[...] = dot(pick[...], ext[0:ATOMS, :]).astype(LOW)

    pl.semaphore_wait(barrier, 8)
    copies1 = [
        push(0, j, send1, ext.at[pl.ds(ATOMS + LIST * (7 - j), LIST), :]) for j in range(8)
    ]
    for copy in copies1:
        copy.start()

    for load in loads[4:]:
        load.wait()
    alive[...] = jnp.where(mask[...] != 0, 1.0 / 16.0, 0.0)
    row_number = lax.broadcasted_iota(jnp.int32, (ROWS, ATOMS), 0)

    def select(c, carry):
        for i in range(PER):
            entry = neighbours[pl.ds(c * PER + i, 1), :]
            entry = jnp.where(entry >= ATOMS + 5 * LIST, entry - LIST, entry)
            here = pl.ds(pl.multiple_of(c * CHUNK + i * ATOMS, ATOMS), ATOMS)
            hot[:, here] = jnp.where(row_number == entry, 1.0, 0.0).astype(LOW)
        return carry

    lax.fori_loop(0, SLOTS // PER, select, 0)
    w1_t[...] = jnp.concatenate(
        [w1[...].astype(F32), jnp.zeros((8, HIDDEN), F32)], axis=0
    ).T.astype(LOW)
    w2_t[...] = w2[...].astype(F32).T.astype(LOW)
    w3_t[...] = w3[...].astype(F32).T.astype(LOW)
    w_a_t[...] = w_a[...].astype(F32).T.astype(LOW)
    w_b_t[...] = w_b[...].astype(F32).T.astype(LOW)
    w_o1_t[...] = w_o1[...].astype(F32).T.astype(LOW)
    features_t[...] = features[...].astype(F32).T
    proj_t[...] = ext[0:ATOMS, 0:CHAN].astype(F32).T
    entry = lax.broadcasted_iota(jnp.int32, (8, ROWS), 1) - ATOMS
    axis = lax.broadcasted_iota(jnp.int32, (8, ROWS), 0)
    block = lax.div(entry + ATOMS, LIST) - ATOMS // LIST
    first = jnp.where(block < 3, -4.0, jnp.where(block > 4, 4.0, 0.0))
    left = (block == 0) | (block == 3) | (block == 5)
    right = (block == 2) | (block == 4) | (block == 7)
    second = jnp.where(left, -4.0, jnp.where(right, 4.0, 0.0))
    offset = jnp.where(axis == 0, first, jnp.where(axis == 1, second, 0.0))
    offset = jnp.where(entry < 0, 0.0, offset)

    for copy in copies1:
        copy.wait_recv()
    ext_t[0:CHAN, :] = ext[:, 0:CHAN].astype(F32).T.astype(LOW)
    pieces_t = ext[:, CHAN : 2 * CHAN].astype(F32).T
    ext_t[CHAN : CHAN + 32, :] = jnp.concatenate([pieces_t[0:24], offset], axis=0).astype(LOW)

    centre = 1.0 + 0.75 * lax.broadcasted_iota(jnp.int32, (8, CHUNK), 0).astype(F32)

    def forward(c, carry):
        here = lanes_of(c)
        found = dot(ext_t[...], hot[:, here])
        partner[:, here] = found[0:CHAN]
        place = found[CHAN : CHAN + 8] + found[CHAN + 8 : CHAN + 16] + found[CHAN + 16 : CHAN + 24]
        place = place + found[CHAN + 24 : CHAN + 32]
        rel = place - jnp.concatenate([own_pos[...]] * PER, axis=1)
        spread = jnp.sqrt(jnp.sum(rel * rel, axis=0, keepdims=True) + 1.0)
        inv = 1.0 / spread
        direction = rel * inv
        unit[:, here] = direction
        inverse[:, here] = jnp.broadcast_to(inv, (8, CHUNK))
        away = spread - centre
        basis = jnp.exp(-(away * away))
        slope[:, here] = -2.0 * away * basis
        wide = jnp.concatenate([basis, jnp.zeros((8, CHUNK), F32)], axis=0).astype(LOW)
        flags = jnp.concatenate([alive[pl.ds(c * PER + i, 1), :] for i in range(PER)], axis=1)
        pre1 = dot(w1_t[...], wide)
        open1 = sigmoid(pre1)
        gate1[:, here] = open1 * (1.0 + pre1 * (1.0 - open1))
        pre2 = dot(w2_t[...], (pre1 * open1).astype(LOW))
        open2 = sigmoid(pre2)
        gate2[:, here] = open2 * (1.0 + pre2 * (1.0 - open2)) * flags
        hid2 = ((pre2 * open2).astype(LOW).astype(F32) * flags).astype(LOW)
        radial[:, here] = dot(w3_t[...], hid2)
        for i in range(PER):
            tile = pl.ds(pl.multiple_of(c * CHUNK + i * ATOMS, ATOMS), ATOMS)
            toward = [-unit[k : k + 1, tile] for k in range(3)]
            for b in range(BANDS):
                rows = pl.ds(b * BAND, BAND)
                own = proj_t[rows, :]
                messages[rows, tile] = (radial[rows, tile] * own).astype(LOW)
                vector = radial[pl.ds(CHAN + b * BAND, BAND), tile] * own
                for k in range(3):
                    messages[pl.ds((k + 1) * CHAN + b * BAND, BAND), tile] = (
                        vector * toward[k]
                    ).astype(LOW)
        return carry

    lax.fori_loop(0, SLOTS // PER, forward, 0)

    send2[...] = dot(hot[ATOMS:ROWS, :], messages[...], NT).astype(LOW)
    copies2 = [
        push(1, j, send2.at[pl.ds(LIST * j, LIST), :], recv2.at[7 - j]) for j in range(8)
    ]
    for copy in copies2:
        copy.start()

    agg[...] = dot(messages[...], hot[0:ATOMS, :], NT)

    def gather_own(c, carry):
        for b in range(BANDS):
            rows = pl.ds(b * BAND, BAND)
            total = [agg[pl.ds(k * CHAN + b * BAND, BAND), :] for k in range(4)]
            for i in range(PER):
                tile = pl.ds(pl.multiple_of(c * CHUNK + i * ATOMS, ATOMS), ATOMS)
                other = partner[rows, tile]
                total[0] = total[0] + radial[rows, tile] * other
                vector = radial[pl.ds(CHAN + b * BAND, BAND), tile] * other
                for k in range(3):
                    total[k + 1] = total[k + 1] + vector * unit[k : k + 1, tile]
            for k in range(4):
                agg[pl.ds(k * CHAN + b * BAND, BAND), :] = total[k]
        return carry

    lax.fori_loop(0, SLOTS // PER, gather_own, 0)

    for copy in copies2:
        copy.wait_recv()
    back = recv2[0].astype(F32)
    for j in range(1, 8):
        back = back + recv2[j].astype(F32)
    twice = jnp.concatenate([pick[...], pick[...]], axis=0)
    agg[...] += dot(jnp.concatenate(split(back.T), axis=1), twice)

    along = [agg[(k + 1) * CHAN : (k + 2) * CHAN, :] for k in range(3)]
    norms = along[0] * along[0] + along[1] * along[1] + along[2] * along[2]
    mixed = features_t[...] + dot(w_a_t[...], agg[0:CHAN, :].astype(LOW))
    mixed = mixed + dot(w_b_t[...], norms.astype(LOW))
    pre = dot(w_o1_t[...], mixed.astype(LOW))
    opened = sigmoid(pre)
    out_weight = column(w_o2[...], 16)
    energies_ref[...] = jnp.sum(pre * opened * out_weight, axis=0, keepdims=True)
    d_pre = out_weight * opened * (1.0 + pre * (1.0 - opened))
    d_mixed = dot(w_o1[...], d_pre.astype(LOW)).astype(LOW)
    cot[0:CHAN, :] = dot(w_a[...], d_mixed).astype(LOW)
    d_norms = 2.0 * dot(w_b[...], d_mixed).astype(LOW).astype(F32)
    for k in range(3):
        cot[(k + 1) * CHAN : (k + 2) * CHAN, :] = (along[k] * d_norms).astype(LOW)
    send3[...] = dot(pick[...], cot[...], NT).astype(LOW)
    copies3 = [push(2, j, send3, recv3.at[pl.ds(LIST * (7 - j), LIST), :]) for j in range(8)]
    for copy in copies3:
        copy.start()
    cot_ext[:, 0:ATOMS] = cot[...]
    for copy in copies3:
        copy.wait_recv()
    cot_ext[:, ATOMS:ROWS] = recv3[...].astype(F32).T.astype(LOW)

    def backward(c, carry):
        here = lanes_of(c)
        partner_cot[...] = dot(cot_ext[...], hot[:, here])
        for i in range(PER):
            tile = pl.ds(pl.multiple_of(c * CHUNK + i * ATOMS, ATOMS), ATOMS)
            inner = pl.ds(i * ATOMS, ATOMS)
            toward = [unit[k : k + 1, tile] for k in range(3)]
            sums = [jnp.zeros((8, ATOMS), F32) for k in range(3)]
            for b in range(BANDS):
                rows = pl.ds(b * BAND, BAND)
                own = proj_t[rows, :]
                other = partner[rows, tile]
                weight = radial[pl.ds(CHAN + b * BAND, BAND), tile]
                d_radial[rows, inner] = (
                    other * cot[rows, :].astype(F32) + own * partner_cot[rows, inner]
                ).astype(LOW)
                flow = jnp.zeros((BAND, ATOMS), F32)
                for k in range(3):
                    part = pl.ds((k + 1) * CHAN + b * BAND, BAND)
                    term = other * cot[part, :].astype(F32) - own * partner_cot[part, inner]
                    flow = flow + toward[k] * term
                    pull = weight * term
                    for r in range(BAND // 8):
                        sums[k] = sums[k] + pull[8 * r : 8 * r + 8]
                d_radial[pl.ds(CHAN + b * BAND, BAND), inner] = flow.astype(LOW)
            for k in range(3):
                d_unit[k : k + 1, inner] = jnp.sum(sums[k], axis=0, keepdims=True)
        d_hid2 = dot(w3[...], d_radial[...])
        d_hid1 = dot(w2[...], (d_hid2 * gate2[:, here]).astype(LOW))
        d_basis = dot(w1[...], (d_hid1 * gate1[:, here]).astype(LOW))
        d_spread = jnp.sum(d_basis * slope[:, here], axis=0, keepdims=True)
        direction = unit[:, here]
        pull = d_unit[...]
        inv = inverse[:, here]
        radial_part = jnp.sum(pull * direction, axis=0, keepdims=True)
        change = (pull - direction * radial_part) * inv + direction * d_spread
        total = carry
        for i in range(PER):
            total = total + change[:, i * ATOMS : (i + 1) * ATOMS]
        d_rel[:, here] = jnp.concatenate(
            [change, change - change.astype(LOW).astype(F32)], axis=0
        ).astype(LOW)
        return total

    d_unit[...] = jnp.zeros_like(d_unit)
    force = lax.fori_loop(0, SLOTS // PER, backward, jnp.zeros((8, ATOMS), F32))

    away = dot(d_rel[...], hot[ATOMS:ROWS, :], NT)
    send4[...] = away[0:8] + away[8:16]
    copies4 = [push(3, j, send4, recv4.at[7 - j]) for j in range(8)]
    for copy in copies4:
        copy.start()
    near = dot(d_rel[...], hot[0:ATOMS, :], NT)
    force = force - (near[0:8] + near[8:16])
    for copy in copies4:
        copy.wait_recv()
    back = recv4[0][:, 7 * LIST : 8 * LIST]
    for j in range(1, 8):
        back = back + recv4[j][:, (7 - j) * LIST : (8 - j) * LIST]
    force = force - dot(jnp.concatenate(split(back), axis=1), twice)
    forces_ref[...] = force[0:3]
    for copy in copies1 + copies2 + copies3 + copies4:
        copy.wait_send()


def body(
    n_dom,
    n_slab,
    features,
    positions,
    neighbours,
    neighbour_mask,
    ghost_list,
    w_up,
    radial_weight_1,
    radial_weight_2,
    radial_weight_3,
    w_a,
    w_b,
    w_o1,
    w_o2,
):
    operands = (
        features,
        positions,
        neighbours,
        neighbour_mask,
        ghost_list.reshape(1, LIST),
        w_up,
        radial_weight_1,
        radial_weight_2,
        radial_weight_3,
        w_a,
        w_b,
        w_o1,
        w_o2.reshape(1, 16),
    )
    held = [pltpu.VMEM(x.shape, x.dtype) for x in operands]
    energies, forces = pl.pallas_call(
        functools.partial(kernel, n_dom, n_slab),
        out_shape=(
            jax.ShapeDtypeStruct((1, ATOMS), F32),
            jax.ShapeDtypeStruct((3, ATOMS), F32),
        ),
        in_specs=[pl.BlockSpec(memory_space=pl.ANY)] * len(operands),
        out_specs=(
            pl.BlockSpec(memory_space=pltpu.VMEM),
            pl.BlockSpec(memory_space=pltpu.VMEM),
        ),
        scratch_shapes=held
        + [
            pltpu.VMEM((ROWS, 2 * CHAN), LOW),
            pltpu.VMEM((CHAN + 32, ROWS), LOW),
            pltpu.VMEM((8, ATOMS), F32),
            pltpu.VMEM((LIST, ATOMS), LOW),
            pltpu.VMEM((SLOTS, ATOMS), F32),
            pltpu.VMEM((ROWS, EDGES), LOW),
            pltpu.VMEM((HIDDEN, 16), LOW),
            pltpu.VMEM((HIDDEN, HIDDEN), LOW),
            pltpu.VMEM((2 * CHAN, HIDDEN), LOW),
            pltpu.VMEM((CHAN, CHAN), LOW),
            pltpu.VMEM((CHAN, CHAN), LOW),
            pltpu.VMEM((16, CHAN), LOW),
            pltpu.VMEM((CHAN, ATOMS), F32),
            pltpu.VMEM((CHAN, ATOMS), F32),
            pltpu.VMEM((CHAN, EDGES), F32),
            pltpu.VMEM((8, EDGES), F32),
            pltpu.VMEM((8, EDGES), F32),
            pltpu.VMEM((8, EDGES), F32),
            pltpu.VMEM((HIDDEN, EDGES), F32),
            pltpu.VMEM((HIDDEN, EDGES), F32),
            pltpu.VMEM((2 * CHAN, EDGES), F32),
            pltpu.VMEM((4 * CHAN, EDGES), LOW),
            pltpu.VMEM((4 * CHAN, ATOMS), F32),
            pltpu.VMEM((4 * CHAN, ATOMS), LOW),
            pltpu.VMEM((4 * CHAN, ROWS), LOW),
            pltpu.VMEM((4 * CHAN, CHUNK), F32),
            pltpu.VMEM((2 * CHAN, CHUNK), LOW),
            pltpu.VMEM((8, CHUNK), F32),
            pltpu.VMEM((16, EDGES), LOW),
            pltpu.VMEM((LIST, 2 * CHAN), LOW),
            pltpu.VMEM((GHOST, 4 * CHAN), LOW),
            pltpu.VMEM((8, LIST, 4 * CHAN), LOW),
            pltpu.VMEM((LIST, 4 * CHAN), LOW),
            pltpu.VMEM((GHOST, 4 * CHAN), LOW),
            pltpu.VMEM((8, GHOST), F32),
            pltpu.VMEM((8, 8, GHOST), F32),
            pltpu.SemaphoreType.DMA((13,)),
            pltpu.SemaphoreType.DMA((4, 8)),
            pltpu.SemaphoreType.DMA((4, 8)),
        ],
        compiler_params=pltpu.CompilerParams(
            collective_id=0, has_side_effects=True, vmem_limit_bytes=48 * 1024 * 1024
        ),
    )(*operands)
    return energies.reshape(ATOMS), forces


def solution(mesh):
    split_rows = P(("dom", "slab"), None)
    split_lanes = P(None, ("dom", "slab"))
    split_flat = P(("dom", "slab"))
    in_specs = (split_rows, split_lanes, split_lanes, split_lanes, split_flat) + (P(),) * 8
    return jax.shard_map(
        functools.partial(body, mesh.shape["dom"], mesh.shape["slab"]),
        mesh=mesh,
        in_specs=in_specs,
        out_specs=(split_flat, split_lanes),
        check_vma=False,
    )
```

```python
import functools

import jax
import jax.numpy as jnp
from jax import lax
from jax.experimental import pallas as pl
from jax.experimental.pallas import tpu as pltpu
from jax.sharding import PartitionSpec as P

MESH = pl.DeviceIdType.MESH
F32 = jnp.float32
LOW = jnp.bfloat16
ATOMS = 128
CHAN = 128
LIST = 32
SLOTS = 32
HIDDEN = 64
GHOST = 8 * LIST
ROWS = ATOMS + GHOST
EDGES = SLOTS * ATOMS
BANDS = 4
BAND = CHAN // BANDS
SIDES = [(a, b) for a in (-1, 0, 1) for b in (-1, 0, 1) if (a, b) != (0, 0)]
ORDER = (0, 2, 5, 7, 1, 6, 3, 4)
NN = (((1,), (0,)), ((), ()))
NT = (((1,), (1,)), ((), ()))


def dot(a, b, dims=NN):
    return lax.dot_general(a, b, dims, preferred_element_type=F32)


def sigmoid(x):
    return 0.5 * jnp.tanh(0.5 * x) + 0.5


def column(row, n):
    down = lax.broadcasted_iota(jnp.int32, (n, n), 0)
    across = lax.broadcasted_iota(jnp.int32, (n, n), 1)
    return jnp.sum(jnp.where(down == across, row, 0.0), axis=1, keepdims=True)


def split(x):
    high = x.astype(LOW)
    return high, (x - high.astype(F32)).astype(LOW)


def tile_of(i):
    return pl.ds(i * ATOMS, ATOMS)


def band(part, b):
    return pl.ds(part * CHAN + b * BAND, BAND)


def fold(x):
    total = x[0:8]
    for r in range(1, x.shape[0] // 8):
        total = total + x[8 * r : 8 * r + 8]
    return total


def kernel(
    n_dom,
    n_slab,
    features_hbm,
    positions_hbm,
    neighbours_hbm,
    mask_hbm,
    list_hbm,
    w_up_hbm,
    w1_hbm,
    w2_hbm,
    w3_hbm,
    w_a_hbm,
    w_b_hbm,
    w_o1_hbm,
    w_o2_hbm,
    energies_ref,
    forces_ref,
    features,
    positions,
    neighbours,
    mask,
    ghost_list,
    w_up,
    w1,
    w2,
    w3,
    w_a,
    w_b,
    w_o1,
    w_o2,
    ext,
    ext_t,
    own_pos,
    pick,
    pick8,
    alive,
    hot,
    w1_t,
    w2_t,
    w3_t,
    w_a_t,
    w_b_t,
    w_o1_t,
    features_t,
    proj_t,
    near_found,
    partner,
    unit,
    inverse,
    slope,
    gate1,
    gate2,
    radial,
    d_radial,
    messages,
    agg,
    cot,
    own_cot,
    partner_cot,
    factors,
    partial,
    send1,
    send2,
    recv2,
    send3,
    recv3,
    send4,
    recv4,
    load_sem,
    out_sem,
    in_sem,
):
    dom = lax.axis_index("dom")
    slab = lax.axis_index("slab")
    peers = [
        (lax.rem(dom + a + n_dom, n_dom), lax.rem(slab + b + n_slab, n_slab)) for a, b in SIDES
    ]
    barrier = pltpu.get_barrier_semaphore()
    for peer in peers:
        pl.semaphore_signal(barrier, inc=1, device_id=peer, device_id_type=MESH)

    def push(phase, j, src, dst):
        return pltpu.make_async_remote_copy(
            src_ref=src,
            dst_ref=dst,
            send_sem=out_sem.at[phase, j],
            recv_sem=in_sem.at[phase, 7 - j],
            device_id=peers[j],
            device_id_type=MESH,
        )

    pairs = [
        (features_hbm, features),
        (w_up_hbm, w_up),
        (positions_hbm, positions),
        (list_hbm, ghost_list),
        (neighbours_hbm, neighbours),
        (mask_hbm, mask),
        (w1_hbm, w1),
        (w2_hbm, w2),
        (w3_hbm, w3),
        (w_a_hbm, w_a),
        (w_b_hbm, w_b),
        (w_o1_hbm, w_o1),
        (w_o2_hbm, w_o2),
    ]
    loads = [pltpu.make_async_copy(a, b, load_sem.at[i]) for i, (a, b) in enumerate(pairs)]
    for load in loads:
        load.start()
    for load in loads[:4]:
        load.wait()

    proj = dot(features[...], w_up[...]).astype(LOW)
    own_pos[...] = jnp.zeros_like(own_pos)
    own_pos[0:3, :] = positions[...]
    coords = own_pos[...]
    high = coords.astype(LOW).astype(F32)
    rest = coords - high
    middle = rest.astype(LOW).astype(F32)
    pieces = jnp.concatenate(
        [high, middle, rest - middle, jnp.zeros((CHAN - 24, ATOMS), F32)], axis=0
    )
    ext[0:ATOMS, 0:CHAN] = proj
    ext[0:ATOMS, CHAN : 2 * CHAN] = pieces.T.astype(LOW)
    list_column = column(ghost_list[...].astype(F32), LIST)
    atom_lane = lax.broadcasted_iota(jnp.int32, (LIST, ATOMS), 1).astype(F32)
    pick[...] = jnp.where(atom_lane == list_column, 1.0, 0.0).astype(LOW)
    send1[...] = dot(pick[...], ext[0:ATOMS, :]).astype(LOW)

    for load in loads[4:]:
        load.wait()
    alive[...] = jnp.where(mask[...] != 0, 1.0 / 16.0, 0.0)
    row_number = lax.broadcasted_iota(jnp.int32, (ROWS, ATOMS), 0)
    for i in range(SLOTS):
        entry = neighbours[i : i + 1, :]
        entry = jnp.where(entry >= ATOMS + 5 * LIST, entry - LIST, entry)
        hot[:, tile_of(i)] = jnp.where(row_number == entry, 1.0, 0.0).astype(LOW)
    w1_t[...] = jnp.concatenate(
        [w1[...].astype(F32), jnp.zeros((8, HIDDEN), F32)], axis=0
    ).T.astype(LOW)
    w2_t[...] = w2[...].astype(F32).T.astype(LOW)
    w3_t[...] = w3[...].astype(F32).T.astype(LOW)
    w_a_t[...] = w_a[...].astype(F32).T.astype(LOW)
    w_b_t[...] = w_b[...].astype(F32).T.astype(LOW)
    w_o1_t[...] = w_o1[...].astype(F32).T.astype(LOW)
    features_t[...] = features[...].astype(F32).T
    own_t = ext[0:ATOMS, :].astype(F32).T
    proj_t[...] = own_t[0:CHAN]
    ext_t[:, 0:ATOMS] = own_t[0 : CHAN + 32].astype(LOW)

    pl.semaphore_wait(barrier, 8)
    copies1 = [
        push(0, j, send1, ext.at[pl.ds(ATOMS + LIST * (7 - j), LIST), :]) for j in range(8)
    ]
    for j in ORDER:
        copies1[j].start()

    near_found[...] = dot(ext_t[:, 0:ATOMS], hot[0:ATOMS, :])
    entry = lax.broadcasted_iota(jnp.int32, (8, GHOST), 1)
    axis = lax.broadcasted_iota(jnp.int32, (8, GHOST), 0)
    block = lax.div(entry, LIST)
    first = jnp.where(block < 3, -4.0, jnp.where(block > 4, 4.0, 0.0))
    left = (block == 0) | (block == 3) | (block == 5)
    right = (block == 2) | (block == 4) | (block == 7)
    second = jnp.where(left, -4.0, jnp.where(right, 4.0, 0.0))
    offset = jnp.where(axis == 0, first, jnp.where(axis == 1, second, 0.0))
    flags = jnp.concatenate([alive[i : i + 1, :] for i in range(SLOTS)], axis=1)
    centre = 1.0 + 0.75 * lax.broadcasted_iota(jnp.int32, (8, EDGES), 0).astype(F32)
    pick8[...] = jnp.concatenate([pick[...]] * 8, axis=0)

    for copy in copies1:
        copy.wait_recv()
    ghost_t = ext[ATOMS:ROWS, :].astype(F32).T
    ext_t[:, ATOMS:ROWS] = jnp.concatenate([ghost_t[0 : CHAN + 24], offset], axis=0).astype(LOW)

    found = near_found[...] + dot(ext_t[:, ATOMS:ROWS], hot[ATOMS:ROWS, :])
    partner[...] = found[0:CHAN]
    place = found[CHAN : CHAN + 8] + found[CHAN + 8 : CHAN + 16] + found[CHAN + 16 : CHAN + 24]
    place = place + found[CHAN + 24 : CHAN + 32]
    rel = place - jnp.concatenate([own_pos[...]] * SLOTS, axis=1)
    spread = jnp.sqrt(jnp.sum(rel * rel, axis=0, keepdims=True) + 1.0)
    inv = 1.0 / spread
    unit[...] = rel * inv
    inverse[...] = jnp.broadcast_to(inv, (8, EDGES))
    away = spread - centre
    basis = jnp.exp(-(away * away))
    slope[...] = -2.0 * away * basis
    blank = jnp.zeros((8, EDGES), F32)
    pre1 = dot(w1_t[...], jnp.concatenate([basis, blank], axis=0).astype(LOW))
    open1 = sigmoid(pre1)
    gate1[...] = open1 * (1.0 + pre1 * (1.0 - open1))
    pre2 = dot(w2_t[...], (pre1 * open1).astype(LOW))
    open2 = sigmoid(pre2)
    gate2[...] = open2 * (1.0 + pre2 * (1.0 - open2)) * flags
    hid2 = ((pre2 * open2).astype(LOW).astype(F32) * flags).astype(LOW)
    radial[...] = dot(w3_t[...], hid2)
    for i in range(SLOTS):
        tile = tile_of(i)
        toward = [-unit[k : k + 1, tile] for k in range(3)]
        for b in range(BANDS):
            own = proj_t[band(0, b), :]
            messages[band(0, b), tile] = (radial[band(0, b), tile] * own).astype(LOW)
            vector = radial[band(1, b), tile] * own
            for k in range(3):
                messages[band(k + 1, b), tile] = (vector * toward[k]).astype(LOW)

    send2[...] = dot(hot[ATOMS:ROWS, :], messages[...], NT).astype(LOW)
    copies2 = [
        push(1, j, send2.at[pl.ds(LIST * j, LIST), :], recv2.at[pl.ds(LIST * (7 - j), LIST), :])
        for j in range(8)
    ]
    for j in ORDER:
        copies2[j].start()

    agg[...] = dot(messages[...], hot[0:ATOMS, :], NT)
    for b in range(BANDS):
        total = [agg[band(k, b), :] for k in range(4)]
        for i in range(SLOTS):
            tile = tile_of(i)
            other = partner[band(0, b), tile]
            total[0] = total[0] + radial[band(0, b), tile] * other
            vector = radial[band(1, b), tile] * other
            for k in range(3):
                total[k + 1] = total[k + 1] + vector * unit[k : k + 1, tile]
        for k in range(4):
            agg[band(k, b), :] = total[k]
    rate = dot(w1_t[...], jnp.concatenate([slope[...], blank], axis=0).astype(LOW))
    rate = dot(w2_t[...], (rate * gate1[...]).astype(LOW))
    d_radial[...] = dot(w3_t[...], (rate * gate2[...]).astype(LOW))

    for copy in copies2:
        copy.wait_recv()
    back = recv2[0:LIST, :].astype(F32)
    for j in range(1, 8):
        back = back + recv2[LIST * j : LIST * (j + 1), :].astype(F32)
    agg[...] += dot(jnp.concatenate(split(back.T), axis=1), pick8[0 : 2 * LIST, :])

    along = [agg[(k + 1) * CHAN : (k + 2) * CHAN, :] for k in range(3)]
    norms = along[0] * along[0] + along[1] * along[1] + along[2] * along[2]
    mixed = features_t[...] + dot(w_a_t[...], agg[0:CHAN, :].astype(LOW))
    mixed = mixed + dot(w_b_t[...], norms.astype(LOW))
    pre = dot(w_o1[...], mixed.astype(LOW))
    opened = sigmoid(pre)
    out_weight = column(w_o2[...], 16)
    energies_ref[...] = jnp.sum(pre * opened * out_weight, axis=0, keepdims=True)
    d_pre = out_weight * opened * (1.0 + pre * (1.0 - opened))
    d_mixed = dot(w_o1_t[...], d_pre.astype(LOW)).astype(LOW)
    cot[0:CHAN, :] = dot(w_a[...], d_mixed).astype(LOW)
    d_norms = 2.0 * dot(w_b[...], d_mixed).astype(LOW).astype(F32)
    for k in range(3):
        cot[(k + 1) * CHAN : (k + 2) * CHAN, :] = (along[k] * d_norms).astype(LOW)
    send3[...] = dot(pick[...], cot[...], NT).astype(LOW)
    copies3 = [push(2, j, send3, recv3.at[pl.ds(LIST * (7 - j), LIST), :]) for j in range(8)]
    for j in ORDER:
        copies3[j].start()

    partner_cot[...] = dot(cot[...], hot[0:ATOMS, :])
    own_cot[...] = cot[...].astype(F32)
    for i in range(SLOTS):
        tile = tile_of(i)
        toward = [unit[k : k + 1, tile] for k in range(3)]
        sums = [jnp.zeros((8, ATOMS), F32) for k in range(4)]
        for b in range(BANDS):
            own = proj_t[band(0, b), :]
            other = partner[band(0, b), tile]
            weight = radial[band(1, b), tile]
            rate_s = d_radial[band(0, b), tile]
            rate_v = d_radial[band(1, b), tile]
            term = other * own_cot[band(0, b), :] + own * partner_cot[band(0, b), tile]
            spread_part = rate_s * term
            flow = jnp.zeros((BAND, ATOMS), F32)
            for k in range(3):
                term = other * own_cot[band(k + 1, b), :] - own * partner_cot[band(k + 1, b), tile]
                flow = flow + toward[k] * term
                sums[k + 1] = sums[k + 1] + fold(weight * term)
            sums[0] = sums[0] + fold(spread_part + rate_v * flow)
            factors[band(0, b), tile] = rate_s * own
            factors[band(1, b), tile] = rate_v * own
            factors[band(2, b), tile] = weight * own
        for k in range(4):
            partial[8 * k : 8 * k + 8, tile] = sums[k]

    for copy in copies3:
        copy.wait_recv()
    ghost_cot = recv3[...].astype(F32).T.astype(LOW)
    partner_cot[...] = dot(ghost_cot, hot[ATOMS:ROWS, :])
    for i in range(SLOTS):
        tile = tile_of(i)
        toward = [unit[k : k + 1, tile] for k in range(3)]
        sums = [partial[8 * k : 8 * k + 8, tile] for k in range(4)]
        for b in range(BANDS):
            weight = factors[band(2, b), tile]
            flow = jnp.zeros((BAND, ATOMS), F32)
            for k in range(3):
                far = partner_cot[band(k + 1, b), tile]
                flow = flow + toward[k] * far
                sums[k + 1] = sums[k + 1] - fold(weight * far)
            spread_part = factors[band(0, b), tile] * partner_cot[band(0, b), tile]
            sums[0] = sums[0] + fold(spread_part - factors[band(1, b), tile] * flow)
        for k in range(4):
            partial[8 * k : 8 * k + 8, tile] = sums[k]
    whole = [jnp.sum(partial[8 * k : 8 * k + 8, :], axis=0, keepdims=True) for k in range(4)]
    direction = unit[...]
    place_row = lax.broadcasted_iota(jnp.int32, (8, EDGES), 0)
    pull = jnp.where(
        place_row == 0,
        whole[1],
        jnp.where(place_row == 1, whole[2], jnp.where(place_row == 2, whole[3], 0.0)),
    )
    lengthwise = jnp.sum(pull * direction, axis=0, keepdims=True)
    change = (pull - direction * lengthwise) * inverse[...] + direction * whole[0]
    high, low = split(change)
    d_rel = jnp.concatenate([high.astype(F32), low.astype(F32)], axis=0).astype(LOW)

    parted = dot(d_rel, hot[ATOMS:ROWS, :], NT)
    send4[...] = parted[0:8] + parted[8:16]
    copies4 = [push(3, j, send4, recv4.at[7 - j]) for j in range(8)]
    for j in ORDER:
        copies4[j].start()
    near = dot(d_rel, hot[0:ATOMS, :], NT)
    force = -(near[0:8] + near[8:16])
    for i in range(SLOTS):
        force = force + change[:, i * ATOMS : (i + 1) * ATOMS]
    for copy in copies4:
        copy.wait_recv()
    lane_block = lax.div(lax.broadcasted_iota(jnp.int32, (8, GHOST), 1), LIST)
    back = recv4[0]
    for j in range(1, 8):
        back = jnp.where(lane_block == 7 - j, recv4[j], back)
    high, low = split(back)
    given = jnp.concatenate([high.astype(F32), low.astype(F32)], axis=0).astype(LOW)
    given = dot(given, pick8[...])
    force = force - (given[0:8] + given[8:16])
    forces_ref[...] = force[0:3]
    for copy in copies1 + copies2 + copies3 + copies4:
        copy.wait_send()


def body(
    n_dom,
    n_slab,
    features,
    positions,
    neighbours,
    neighbour_mask,
    ghost_list,
    w_up,
    radial_weight_1,
    radial_weight_2,
    radial_weight_3,
    w_a,
    w_b,
    w_o1,
    w_o2,
):
    operands = (
        features,
        positions,
        neighbours,
        neighbour_mask,
        ghost_list.reshape(1, LIST),
        w_up,
        radial_weight_1,
        radial_weight_2,
        radial_weight_3,
        w_a,
        w_b,
        w_o1.T,
        w_o2.reshape(1, 16),
    )
    held = [pltpu.VMEM(x.shape, x.dtype) for x in operands]
    energies, forces = pl.pallas_call(
        functools.partial(kernel, n_dom, n_slab),
        out_shape=(
            jax.ShapeDtypeStruct((1, ATOMS), F32),
            jax.ShapeDtypeStruct((3, ATOMS), F32),
        ),
        in_specs=[pl.BlockSpec(memory_space=pltpu.HBM)] * len(operands),
        out_specs=(
            pl.BlockSpec(memory_space=pltpu.VMEM),
            pl.BlockSpec(memory_space=pltpu.VMEM),
        ),
        scratch_shapes=held
        + [
            pltpu.VMEM((ROWS, 2 * CHAN), LOW),
            pltpu.VMEM((CHAN + 32, ROWS), LOW),
            pltpu.VMEM((8, ATOMS), F32),
            pltpu.VMEM((LIST, ATOMS), LOW),
            pltpu.VMEM((GHOST, ATOMS), LOW),
            pltpu.VMEM((SLOTS, ATOMS), F32),
            pltpu.VMEM((ROWS, EDGES), LOW),
            pltpu.VMEM((HIDDEN, 16), LOW),
            pltpu.VMEM((HIDDEN, HIDDEN), LOW),
            pltpu.VMEM((2 * CHAN, HIDDEN), LOW),
            pltpu.VMEM((CHAN, CHAN), LOW),
            pltpu.VMEM((CHAN, CHAN), LOW),
            pltpu.VMEM((CHAN, 16), LOW),
            pltpu.VMEM((CHAN, ATOMS), F32),
            pltpu.VMEM((CHAN, ATOMS), F32),
            pltpu.VMEM((CHAN + 32, EDGES), F32),
            pltpu.VMEM((CHAN, EDGES), F32),
            pltpu.VMEM((8, EDGES), F32),
            pltpu.VMEM((8, EDGES), F32),
            pltpu.VMEM((8, EDGES), F32),
            pltpu.VMEM((HIDDEN, EDGES), F32),
            pltpu.VMEM((HIDDEN, EDGES), F32),
            pltpu.VMEM((2 * CHAN, EDGES), F32),
            pltpu.VMEM((2 * CHAN, EDGES), F32),
            pltpu.VMEM((4 * CHAN, EDGES), LOW),
            pltpu.VMEM((4 * CHAN, ATOMS), F32),
            pltpu.VMEM((4 * CHAN, ATOMS), LOW),
            pltpu.VMEM((4 * CHAN, ATOMS), F32),
            pltpu.VMEM((4 * CHAN, EDGES), F32),
            pltpu.VMEM((3 * CHAN, EDGES), F32),
            pltpu.VMEM((32, EDGES), F32),
            pltpu.VMEM((LIST, 2 * CHAN), LOW),
            pltpu.VMEM((GHOST, 4 * CHAN), LOW),
            pltpu.VMEM((GHOST, 4 * CHAN), LOW),
            pltpu.VMEM((LIST, 4 * CHAN), LOW),
            pltpu.VMEM((GHOST, 4 * CHAN), LOW),
            pltpu.VMEM((8, GHOST), F32),
            pltpu.VMEM((8, 8, GHOST), F32),
            pltpu.SemaphoreType.DMA((13,)),
            pltpu.SemaphoreType.DMA((4, 8)),
            pltpu.SemaphoreType.DMA((4, 8)),
        ],
        compiler_params=pltpu.CompilerParams(
            collective_id=0, has_side_effects=True, vmem_limit_bytes=64 * 1024 * 1024
        ),
    )(*operands)
    return energies.reshape(ATOMS), forces


def solution(mesh):
    split_rows = P(("dom", "slab"), None)
    split_lanes = P(None, ("dom", "slab"))
    split_flat = P(("dom", "slab"))
    in_specs = (split_rows, split_lanes, split_lanes, split_lanes, split_flat) + (P(),) * 8
    return jax.shard_map(
        functools.partial(body, mesh.shape["dom"], mesh.shape["slab"]),
        mesh=mesh,
        in_specs=in_specs,
        out_specs=(split_flat, split_lanes),
        check_vma=False,
    )
```

```python
import functools

import jax
import jax.numpy as jnp
from jax import lax
from jax.experimental import pallas as pl
from jax.experimental.pallas import tpu as pltpu
from jax.sharding import PartitionSpec as P

MESH = pl.DeviceIdType.MESH
F32 = jnp.float32
LOW = jnp.bfloat16
ATOMS = 128
CHAN = 128
LIST = 32
SLOTS = 32
HIDDEN = 64
GHOST = 8 * LIST
ROWS = ATOMS + GHOST
EDGES = SLOTS * ATOMS
BANDS = 4
BAND = CHAN // BANDS
SIDES = [(a, b) for a in (-1, 0, 1) for b in (-1, 0, 1) if (a, b) != (0, 0)]
ORDER = (0, 2, 5, 7, 1, 6, 3, 4)
NN = (((1,), (0,)), ((), ()))
NT = (((1,), (1,)), ((), ()))


def dot(a, b, dims=NN):
    return lax.dot_general(a, b, dims, preferred_element_type=F32)


def sigmoid(x):
    return 0.5 * jnp.tanh(0.5 * x) + 0.5


def slope_of(x):
    opened = sigmoid(x)
    return opened * (1.0 + x * (1.0 - opened))


def column(row, n):
    down = lax.broadcasted_iota(jnp.int32, (n, n), 0)
    across = lax.broadcasted_iota(jnp.int32, (n, n), 1)
    return jnp.sum(jnp.where(down == across, row, 0.0), axis=1, keepdims=True)


def split(x):
    high = x.astype(LOW)
    return high, (x - high.astype(F32)).astype(LOW)


def tile_of(i):
    return pl.ds(i * ATOMS, ATOMS)


def band(part, b):
    return pl.ds(part * CHAN + b * BAND, BAND)


def fold(x):
    total = x[0:8]
    for r in range(1, x.shape[0] // 8):
        total = total + x[8 * r : 8 * r + 8]
    return total


def kernel(
    n_dom,
    n_slab,
    features_hbm,
    positions_hbm,
    neighbours_hbm,
    mask_hbm,
    list_hbm,
    w_up_hbm,
    w1_hbm,
    w2_hbm,
    w3_hbm,
    w_a_hbm,
    w_b_hbm,
    w_o1_hbm,
    w_o2_hbm,
    energies_ref,
    forces_ref,
    features,
    positions,
    neighbours,
    mask,
    ghost_list,
    w_up,
    w1,
    w2,
    w3,
    w_a,
    w_b,
    w_o1,
    w_o2,
    ext,
    ext_t,
    own_pos,
    pick,
    pick8,
    alive,
    hot,
    w1_t,
    w2_t,
    w3_t,
    fold_rows,
    fold_columns,
    own_pre,
    out_weight,
    proj_t,
    near_found,
    partner,
    unit,
    inverse,
    slope,
    gate1,
    gate2,
    radial,
    d_radial,
    messages,
    agg,
    cot,
    own_cot,
    partner_cot,
    factors,
    partial,
    send1,
    send2,
    recv2,
    send3,
    recv3,
    send4,
    recv4,
    load_sem,
    out_sem,
    in_sem,
):
    dom = lax.axis_index("dom")
    slab = lax.axis_index("slab")
    peers = [
        (lax.rem(dom + a + n_dom, n_dom), lax.rem(slab + b + n_slab, n_slab)) for a, b in SIDES
    ]
    barrier = pltpu.get_barrier_semaphore()
    for peer in peers:
        pl.semaphore_signal(barrier, inc=1, device_id=peer, device_id_type=MESH)

    def push(phase, j, src, dst):
        return pltpu.make_async_remote_copy(
            src_ref=src,
            dst_ref=dst,
            send_sem=out_sem.at[phase, j],
            recv_sem=in_sem.at[phase, 7 - j],
            device_id=peers[j],
            device_id_type=MESH,
        )

    pairs = [
        (features_hbm, features),
        (w_up_hbm, w_up),
        (positions_hbm, positions),
        (list_hbm, ghost_list),
        (neighbours_hbm, neighbours),
        (mask_hbm, mask),
        (w1_hbm, w1),
        (w2_hbm, w2),
        (w3_hbm, w3),
        (w_a_hbm, w_a),
        (w_b_hbm, w_b),
        (w_o1_hbm, w_o1),
        (w_o2_hbm, w_o2),
    ]
    loads = [pltpu.make_async_copy(a, b, load_sem.at[i]) for i, (a, b) in enumerate(pairs)]
    for load in loads:
        load.start()
    for load in loads[:4]:
        load.wait()

    proj = dot(features[...], w_up[...]).astype(LOW)
    own_pos[...] = jnp.zeros_like(own_pos)
    own_pos[0:3, :] = positions[...]
    coords = own_pos[...]
    high = coords.astype(LOW).astype(F32)
    rest = coords - high
    middle = rest.astype(LOW).astype(F32)
    pieces = jnp.concatenate(
        [high, middle, rest - middle, jnp.zeros((CHAN - 24, ATOMS), F32)], axis=0
    )
    ext[0:ATOMS, 0:CHAN] = proj
    ext[0:ATOMS, CHAN : 2 * CHAN] = pieces.T.astype(LOW)
    list_column = column(ghost_list[...].astype(F32), LIST)
    atom_lane = lax.broadcasted_iota(jnp.int32, (LIST, ATOMS), 1).astype(F32)
    pick[...] = jnp.where(atom_lane == list_column, 1.0, 0.0).astype(LOW)
    send1[...] = dot(pick[...], ext[0:ATOMS, :]).astype(LOW)

    for load in loads[4:]:
        load.wait()
    alive[...] = jnp.where(mask[...] != 0, 1.0 / 16.0, 0.0)
    row_number = lax.broadcasted_iota(jnp.int32, (ROWS, ATOMS), 0)
    for i in range(SLOTS):
        entry = neighbours[i : i + 1, :]
        entry = jnp.where(entry >= ATOMS + 5 * LIST, entry - LIST, entry)
        hot[:, tile_of(i)] = jnp.where(row_number == entry, 1.0, 0.0).astype(LOW)
    w1_t[...] = jnp.concatenate(
        [w1[...].astype(F32), jnp.zeros((8, HIDDEN), F32)], axis=0
    ).T.astype(LOW)
    w2_t[...] = w2[...].astype(F32).T.astype(LOW)
    w3_t[...] = w3[...].astype(F32).T.astype(LOW)
    own_t = ext[0:ATOMS, :].astype(F32).T
    proj_t[...] = own_t[0:CHAN]
    ext_t[:, 0:ATOMS] = own_t[0 : CHAN + 32].astype(LOW)

    pl.semaphore_wait(barrier, 8)
    copies1 = [
        push(0, j, send1, ext.at[pl.ds(ATOMS + LIST * (7 - j), LIST), :]) for j in range(8)
    ]
    for j in ORDER:
        copies1[j].start()

    folded = jnp.concatenate([dot(w_o1[...], w_a[...], NT), dot(w_o1[...], w_b[...], NT)], axis=1)
    high, low = split(folded)
    folded = jnp.concatenate([high.astype(F32), low.astype(F32)], axis=0)
    fold_rows[...] = folded.astype(LOW)
    fold_columns[...] = folded.T.astype(LOW)
    own_pre[...] = dot(w_o1[...], features[...], NT)
    out_weight[...] = column(w_o2[...], 16)
    near_found[...] = dot(ext_t[CHAN : CHAN + 32, 0:ATOMS], hot[0:ATOMS, :])
    entry = lax.broadcasted_iota(jnp.int32, (8, GHOST), 1)
    axis = lax.broadcasted_iota(jnp.int32, (8, GHOST), 0)
    block = lax.div(entry, LIST)
    first = jnp.where(block < 3, -4.0, jnp.where(block > 4, 4.0, 0.0))
    left = (block == 0) | (block == 3) | (block == 5)
    right = (block == 2) | (block == 4) | (block == 7)
    second = jnp.where(left, -4.0, jnp.where(right, 4.0, 0.0))
    offset = jnp.where(axis == 0, first, jnp.where(axis == 1, second, 0.0))
    flags = jnp.concatenate([alive[i : i + 1, :] for i in range(SLOTS)], axis=1)
    centre = 1.0 + 0.75 * lax.broadcasted_iota(jnp.int32, (8, EDGES), 0).astype(F32)
    pick8[...] = jnp.concatenate([pick[...]] * 8, axis=0)

    for copy in copies1:
        copy.wait_recv()
    ghost_t = ext[ATOMS:ROWS, :].astype(F32).T
    ext_t[:, ATOMS:ROWS] = jnp.concatenate([ghost_t[0 : CHAN + 24], offset], axis=0).astype(LOW)

    found = near_found[...] + dot(ext_t[CHAN : CHAN + 32, ATOMS:ROWS], hot[ATOMS:ROWS, :])
    place = found[0:8] + found[8:16] + found[16:24] + found[24:32]
    unit[...] = place - jnp.concatenate([own_pos[...]] * SLOTS, axis=1)
    rel = [jnp.broadcast_to(unit[k : k + 1, :], (8, EDGES)) for k in range(3)]
    spread = jnp.sqrt(rel[0] * rel[0] + rel[1] * rel[1] + rel[2] * rel[2] + 1.0)
    inverse[...] = 1.0 / spread
    unit[...] = unit[...] * inverse[...]
    away = spread - centre
    basis = jnp.exp(-(away * away))
    slope[...] = -2.0 * away * basis
    blank = jnp.zeros((8, EDGES), F32)
    pre1 = dot(w1_t[...], jnp.concatenate([basis, blank], axis=0).astype(LOW))
    open1 = sigmoid(pre1)
    gate1[...] = pre1
    pre2 = dot(w2_t[...], (pre1 * open1).astype(LOW))
    open2 = sigmoid(pre2)
    gate2[...] = pre2
    hid2 = ((pre2 * open2).astype(LOW).astype(F32) * flags).astype(LOW)
    radial[...] = dot(w3_t[...], hid2)
    for i in range(SLOTS):
        tile = tile_of(i)
        toward = [-unit[k : k + 1, tile] for k in range(3)]
        for b in range(BANDS):
            own = proj_t[band(0, b), :]
            messages[band(0, b), tile] = (radial[band(0, b), tile] * own).astype(LOW)
            vector = radial[band(1, b), tile] * own
            for k in range(3):
                messages[band(k + 1, b), tile] = (vector * toward[k]).astype(LOW)

    send2[...] = dot(hot[ATOMS:ROWS, :], messages[...], NT).astype(LOW)
    copies2 = [
        push(1, j, send2.at[pl.ds(LIST * j, LIST), :], recv2.at[pl.ds(LIST * (7 - j), LIST), :])
        for j in range(8)
    ]
    for j in ORDER:
        copies2[j].start()

    partner[...] = dot(ext_t[0:CHAN, :], hot[...])
    agg[...] = dot(messages[...], hot[0:ATOMS, :], NT)
    for b in range(BANDS):
        total = [agg[band(k, b), :] for k in range(4)]
        for i in range(SLOTS):
            tile = tile_of(i)
            other = partner[band(0, b), tile]
            total[0] = total[0] + radial[band(0, b), tile] * other
            vector = radial[band(1, b), tile] * other
            for k in range(3):
                total[k + 1] = total[k + 1] + vector * unit[k : k + 1, tile]
        for k in range(4):
            agg[band(k, b), :] = total[k]
    rate = dot(w1_t[...], jnp.concatenate([slope[...], blank], axis=0).astype(LOW))
    rate = dot(w2_t[...], (rate * slope_of(gate1[...])).astype(LOW))
    rate = rate * slope_of(gate2[...]) * flags
    d_radial[...] = dot(w3_t[...], rate.astype(LOW))

    for copy in copies2:
        copy.wait_recv()
    back = recv2[0:LIST, :].astype(F32)
    for j in range(1, 8):
        back = back + recv2[LIST * j : LIST * (j + 1), :].astype(F32)
    agg[...] += dot(jnp.concatenate(split(back.T), axis=1), pick8[0 : 2 * LIST, :])

    along = [agg[(k + 1) * CHAN : (k + 2) * CHAN, :] for k in range(3)]
    norms = along[0] * along[0] + along[1] * along[1] + along[2] * along[2]
    lowered = jnp.concatenate([agg[0:CHAN, :].astype(LOW), norms.astype(LOW)], axis=0)
    pre = dot(fold_rows[...], lowered)
    pre = pre[0:16] + pre[16:32] + own_pre[...]
    opened = sigmoid(pre)
    energies_ref[...] = jnp.sum(pre * opened * out_weight[...], axis=0, keepdims=True)
    d_pre = out_weight[...] * opened * (1.0 + pre * (1.0 - opened))
    d_pre = d_pre.astype(LOW)
    back = dot(fold_columns[...], jnp.concatenate([d_pre, d_pre], axis=0))
    cot[0:CHAN, :] = back[0:CHAN].astype(LOW)
    d_norms = 2.0 * back[CHAN : 2 * CHAN]
    for k in range(3):
        cot[(k + 1) * CHAN : (k + 2) * CHAN, :] = (along[k] * d_norms).astype(LOW)
    send3[...] = dot(pick[...], cot[...], NT).astype(LOW)
    copies3 = [push(2, j, send3, recv3.at[pl.ds(LIST * (7 - j), LIST), :]) for j in range(8)]
    for j in ORDER:
        copies3[j].start()

    partner_cot[...] = dot(cot[...], hot[0:ATOMS, :])
    own_cot[...] = cot[...].astype(F32)
    for i in range(SLOTS):
        tile = tile_of(i)
        toward = [unit[k : k + 1, tile] for k in range(3)]
        sums = [jnp.zeros((8, ATOMS), F32) for k in range(4)]
        for b in range(BANDS):
            own = proj_t[band(0, b), :]
            other = partner[band(0, b), tile]
            weight = radial[band(1, b), tile]
            rate_s = d_radial[band(0, b), tile]
            rate_v = d_radial[band(1, b), tile]
            term = other * own_cot[band(0, b), :] + own * partner_cot[band(0, b), tile]
            spread_part = rate_s * term
            flow = jnp.zeros((BAND, ATOMS), F32)
            for k in range(3):
                term = other * own_cot[band(k + 1, b), :] - own * partner_cot[band(k + 1, b), tile]
                flow = flow + toward[k] * term
                sums[k + 1] = sums[k + 1] + fold(weight * term)
            sums[0] = sums[0] + fold(spread_part + rate_v * flow)
            factors[band(0, b), tile] = rate_s * own
            factors[band(1, b), tile] = rate_v * own
            factors[band(2, b), tile] = weight * own
        for k in range(4):
            partial[8 * k : 8 * k + 8, tile] = sums[k]

    for copy in copies3:
        copy.wait_recv()
    ghost_cot = recv3[...].astype(F32).T.astype(LOW)
    partner_cot[...] = dot(ghost_cot, hot[ATOMS:ROWS, :])
    for i in range(SLOTS):
        tile = tile_of(i)
        toward = [unit[k : k + 1, tile] for k in range(3)]
        sums = [partial[8 * k : 8 * k + 8, tile] for k in range(4)]
        for b in range(BANDS):
            weight = factors[band(2, b), tile]
            flow = jnp.zeros((BAND, ATOMS), F32)
            for k in range(3):
                far = partner_cot[band(k + 1, b), tile]
                flow = flow + toward[k] * far
                sums[k + 1] = sums[k + 1] - fold(weight * far)
            spread_part = factors[band(0, b), tile] * partner_cot[band(0, b), tile]
            sums[0] = sums[0] + fold(spread_part - factors[band(1, b), tile] * flow)
        for k in range(4):
            partial[8 * k : 8 * k + 8, tile] = sums[k]
    high, low = split(partial[...])
    halves = jnp.concatenate([high, low], axis=0)
    row = lax.broadcasted_iota(jnp.int32, (32, 64), 0)
    across = lax.broadcasted_iota(jnp.int32, (32, 64), 1)
    same = lax.div(row, 8) == lax.rem(lax.div(across, 8), 4)
    whole = dot(jnp.where(same, 1.0, 0.0).astype(LOW), halves)
    along = [unit[k : k + 1, :] for k in range(3)]
    lengthwise = whole[8:16] * along[0] + whole[16:24] * along[1] + whole[24:32] * along[2]
    place_row = lax.broadcasted_iota(jnp.int32, (8, EDGES), 0)
    pull = jnp.where(place_row == 2, whole[24:32], 0.0)
    pull = jnp.where(place_row == 1, whole[16:24], pull)
    pull = jnp.where(place_row == 0, whole[8:16], pull)
    change = (pull - unit[...] * lengthwise) * inverse[...] + unit[...] * whole[0:8]
    high, low = split(change)
    d_rel = jnp.concatenate([high.astype(F32), low.astype(F32)], axis=0).astype(LOW)

    parted = dot(d_rel, hot[ATOMS:ROWS, :], NT)
    send4[...] = parted[0:8] + parted[8:16]
    copies4 = [push(3, j, send4, recv4.at[7 - j]) for j in range(8)]
    for j in ORDER:
        copies4[j].start()
    near = dot(d_rel, hot[0:ATOMS, :], NT)
    force = -(near[0:8] + near[8:16])
    for i in range(SLOTS):
        force = force + change[:, i * ATOMS : (i + 1) * ATOMS]
    for copy in copies4:
        copy.wait_recv()
    lane_block = lax.div(lax.broadcasted_iota(jnp.int32, (8, GHOST), 1), LIST)
    back = recv4[0]
    for j in range(1, 8):
        back = jnp.where(lane_block == 7 - j, recv4[j], back)
    high, low = split(back)
    given = jnp.concatenate([high.astype(F32), low.astype(F32)], axis=0).astype(LOW)
    given = dot(given, pick8[...])
    force = force - (given[0:8] + given[8:16])
    forces_ref[...] = force[0:3]
    for copy in copies1 + copies2 + copies3 + copies4:
        copy.wait_send()


def body(
    n_dom,
    n_slab,
    features,
    positions,
    neighbours,
    neighbour_mask,
    ghost_list,
    w_up,
    radial_weight_1,
    radial_weight_2,
    radial_weight_3,
    w_a,
    w_b,
    w_o1,
    w_o2,
):
    operands = (
        features,
        positions,
        neighbours,
        neighbour_mask,
        ghost_list.reshape(1, LIST),
        w_up,
        radial_weight_1,
        radial_weight_2,
        radial_weight_3,
        w_a,
        w_b,
        w_o1.T,
        w_o2.reshape(1, 16),
    )
    operands = tuple(pltpu.with_memory_space_constraint(x, pltpu.HBM) for x in operands)
    held = [pltpu.VMEM(x.shape, x.dtype) for x in operands]
    energies, forces = pl.pallas_call(
        functools.partial(kernel, n_dom, n_slab),
        out_shape=(
            pltpu.VMEM((1, ATOMS), F32),
            pltpu.VMEM((3, ATOMS), F32),
        ),
        in_specs=[pl.BlockSpec(memory_space=pltpu.HBM)] * len(operands),
        out_specs=(
            pl.BlockSpec(memory_space=pltpu.VMEM),
            pl.BlockSpec(memory_space=pltpu.VMEM),
        ),
        scratch_shapes=held
        + [
            pltpu.VMEM((ROWS, 2 * CHAN), LOW),
            pltpu.VMEM((CHAN + 32, ROWS), LOW),
            pltpu.VMEM((8, ATOMS), F32),
            pltpu.VMEM((LIST, ATOMS), LOW),
            pltpu.VMEM((GHOST, ATOMS), LOW),
            pltpu.VMEM((SLOTS, ATOMS), F32),
            pltpu.VMEM((ROWS, EDGES), LOW),
            pltpu.VMEM((HIDDEN, 16), LOW),
            pltpu.VMEM((HIDDEN, HIDDEN), LOW),
            pltpu.VMEM((2 * CHAN, HIDDEN), LOW),
            pltpu.VMEM((32, 2 * CHAN), LOW),
            pltpu.VMEM((2 * CHAN, 32), LOW),
            pltpu.VMEM((16, ATOMS), F32),
            pltpu.VMEM((16, 1), F32),
            pltpu.VMEM((CHAN, ATOMS), F32),
            pltpu.VMEM((32, EDGES), F32),
            pltpu.VMEM((CHAN, EDGES), F32),
            pltpu.VMEM((8, EDGES), F32),
            pltpu.VMEM((8, EDGES), F32),
            pltpu.VMEM((8, EDGES), F32),
            pltpu.VMEM((HIDDEN, EDGES), F32),
            pltpu.VMEM((HIDDEN, EDGES), F32),
            pltpu.VMEM((2 * CHAN, EDGES), F32),
            pltpu.VMEM((2 * CHAN, EDGES), F32),
            pltpu.VMEM((4 * CHAN, EDGES), LOW),
            pltpu.VMEM((4 * CHAN, ATOMS), F32),
            pltpu.VMEM((4 * CHAN, ATOMS), LOW),
            pltpu.VMEM((4 * CHAN, ATOMS), F32),
            pltpu.VMEM((4 * CHAN, EDGES), F32),
            pltpu.VMEM((3 * CHAN, EDGES), F32),
            pltpu.VMEM((32, EDGES), F32),
            pltpu.VMEM((LIST, 2 * CHAN), LOW),
            pltpu.VMEM((GHOST, 4 * CHAN), LOW),
            pltpu.VMEM((GHOST, 4 * CHAN), LOW),
            pltpu.VMEM((LIST, 4 * CHAN), LOW),
            pltpu.VMEM((GHOST, 4 * CHAN), LOW),
            pltpu.VMEM((8, GHOST), F32),
            pltpu.VMEM((8, 8, GHOST), F32),
            pltpu.SemaphoreType.DMA((13,)),
            pltpu.SemaphoreType.DMA((4, 8)),
            pltpu.SemaphoreType.DMA((4, 8)),
        ],
        compiler_params=pltpu.CompilerParams(
            collective_id=0, has_side_effects=True, vmem_limit_bytes=48 * 1024 * 1024
        ),
    )(*operands)
    return energies.reshape(ATOMS), forces


def solution(mesh):
    split_rows = P(("dom", "slab"), None)
    split_lanes = P(None, ("dom", "slab"))
    split_flat = P(("dom", "slab"))
    in_specs = (split_rows, split_lanes, split_lanes, split_lanes, split_flat) + (P(),) * 8
    return jax.shard_map(
        functools.partial(body, mesh.shape["dom"], mesh.shape["slab"]),
        mesh=mesh,
        in_specs=in_specs,
        out_specs=(split_flat, split_lanes),
        check_vma=False,
    )
```

```python
import functools

import jax
import jax.numpy as jnp
from jax import lax
from jax.experimental import pallas as pl
from jax.experimental.pallas import tpu as pltpu
from jax.sharding import PartitionSpec as P

MESH = pl.DeviceIdType.MESH
F32 = jnp.float32
LOW = jnp.bfloat16
ATOMS = 128
CHAN = 128
LIST = 32
SLOTS = 32
HIDDEN = 64
GHOST = 8 * LIST
ROWS = ATOMS + GHOST
EDGES = SLOTS * ATOMS
BANDS = 4
BAND = CHAN // BANDS
SIDES = [(a, b) for a in (-1, 0, 1) for b in (-1, 0, 1) if (a, b) != (0, 0)]
ORDER = (0, 2, 5, 7, 1, 6, 3, 4)
NN = (((1,), (0,)), ((), ()))
NT = (((1,), (1,)), ((), ()))


def dot(a, b, dims=NN):
    return lax.dot_general(a, b, dims, preferred_element_type=F32)


def sigmoid(x):
    return 0.5 * jnp.tanh(0.5 * x) + 0.5


def slope_of(x):
    opened = sigmoid(x)
    return opened * (1.0 + x * (1.0 - opened))


def column(row, n):
    down = lax.broadcasted_iota(jnp.int32, (n, n), 0)
    across = lax.broadcasted_iota(jnp.int32, (n, n), 1)
    return jnp.sum(jnp.where(down == across, row, 0.0), axis=1, keepdims=True)


def split(x):
    high = x.astype(LOW)
    return high, (x - high.astype(F32)).astype(LOW)


def tile_of(i):
    return pl.ds(i * ATOMS, ATOMS)


def band(part, b):
    return pl.ds(part * CHAN + b * BAND, BAND)


def fold(x):
    total = x[0:8]
    for r in range(1, x.shape[0] // 8):
        total = total + x[8 * r : 8 * r + 8]
    return total


def kernel(
    n_dom,
    n_slab,
    features_hbm,
    positions_hbm,
    neighbours_hbm,
    mask_hbm,
    list_hbm,
    w_up_hbm,
    w1_hbm,
    w2_hbm,
    w3_hbm,
    w_a_hbm,
    w_b_hbm,
    w_o1_hbm,
    w_o2_hbm,
    energies_ref,
    forces_ref,
    features,
    positions,
    neighbours,
    mask,
    ghost_list,
    w_up,
    w1,
    w2,
    w3,
    w_a,
    w_b,
    w_o1,
    w_o2,
    ext,
    ext_t,
    own_pos,
    pick,
    pick8,
    alive,
    hot,
    w1_t,
    w2_t,
    w3_t,
    fold_rows,
    fold_columns,
    own_pre,
    out_weight,
    proj_t,
    near_found,
    partner,
    unit,
    inverse,
    slope,
    gate1,
    gate2,
    radial,
    d_radial,
    messages,
    agg,
    cot,
    own_cot,
    partner_cot,
    factors,
    partial,
    send1,
    send2,
    recv2,
    send3,
    recv3,
    send4,
    recv4,
    load_sem,
    out_sem,
    in_sem,
):
    dom = lax.axis_index("dom")
    slab = lax.axis_index("slab")
    peers = [
        (lax.rem(dom + a + n_dom, n_dom), lax.rem(slab + b + n_slab, n_slab)) for a, b in SIDES
    ]
    barrier = pltpu.get_barrier_semaphore()
    for peer in peers:
        pl.semaphore_signal(barrier, inc=1, device_id=peer, device_id_type=MESH)

    def push(phase, j, src, dst):
        return pltpu.make_async_remote_copy(
            src_ref=src,
            dst_ref=dst,
            send_sem=out_sem.at[phase, j],
            recv_sem=in_sem.at[phase, 7 - j],
            device_id=peers[j],
            device_id_type=MESH,
        )

    pairs = [
        (features_hbm, features),
        (w_up_hbm, w_up),
        (positions_hbm, positions),
        (list_hbm, ghost_list),
        (neighbours_hbm, neighbours),
        (mask_hbm, mask),
        (w1_hbm, w1),
        (w2_hbm, w2),
        (w3_hbm, w3),
        (w_a_hbm, w_a),
        (w_b_hbm, w_b),
        (w_o1_hbm, w_o1),
        (w_o2_hbm, w_o2),
    ]
    loads = [pltpu.make_async_copy(a, b, load_sem.at[i]) for i, (a, b) in enumerate(pairs)]
    for load in loads:
        load.start()
    for load in loads[:4]:
        load.wait()

    proj = dot(features[...], w_up[...]).astype(LOW)
    own_pos[...] = jnp.zeros_like(own_pos)
    own_pos[0:3, :] = positions[...]
    coords = own_pos[...]
    high = coords.astype(LOW).astype(F32)
    rest = coords - high
    middle = rest.astype(LOW).astype(F32)
    pieces = jnp.concatenate(
        [high, middle, rest - middle, jnp.zeros((CHAN - 24, ATOMS), F32)], axis=0
    )
    ext[0:ATOMS, 0:CHAN] = proj
    ext[0:ATOMS, CHAN : 2 * CHAN] = pieces.T.astype(LOW)
    list_column = column(ghost_list[...].astype(F32), LIST)
    atom_lane = lax.broadcasted_iota(jnp.int32, (LIST, ATOMS), 1).astype(F32)
    pick[...] = jnp.where(atom_lane == list_column, 1.0, 0.0).astype(LOW)
    send1[...] = dot(pick[...], ext[0:ATOMS, :]).astype(LOW)

    for load in loads[4:]:
        load.wait()
    alive[...] = jnp.where(mask[...] != 0, 1.0 / 16.0, 0.0)
    row_number = lax.broadcasted_iota(jnp.int32, (ROWS, ATOMS), 0)
    for i in range(SLOTS):
        entry = neighbours[i : i + 1, :]
        entry = jnp.where(entry >= ATOMS + 5 * LIST, entry - LIST, entry)
        hot[:, tile_of(i)] = jnp.where(row_number == entry, 1.0, 0.0).astype(LOW)
    w1_t[...] = jnp.concatenate(
        [w1[...].astype(F32), jnp.zeros((8, HIDDEN), F32)], axis=0
    ).T.astype(LOW)
    w2_t[...] = w2[...].astype(F32).T.astype(LOW)
    w3_t[...] = w3[...].astype(F32).T.astype(LOW)
    own_t = ext[0:ATOMS, :].astype(F32).T
    proj_t[...] = own_t[0:CHAN]
    ext_t[:, 0:ATOMS] = own_t[0 : CHAN + 32].astype(LOW)

    pl.semaphore_wait(barrier, 8)
    copies1 = [
        push(0, j, send1, ext.at[pl.ds(ATOMS + LIST * (7 - j), LIST), :]) for j in range(8)
    ]
    for j in ORDER:
        copies1[j].start()

    folded = jnp.concatenate([dot(w_o1[...], w_a[...], NT), dot(w_o1[...], w_b[...], NT)], axis=1)
    high, low = split(folded)
    folded = jnp.concatenate([high.astype(F32), low.astype(F32)], axis=0)
    fold_rows[...] = folded.astype(LOW)
    fold_columns[...] = folded.T.astype(LOW)
    own_pre[...] = dot(w_o1[...], features[...], NT)
    out_weight[...] = column(w_o2[...], 16)
    near_found[...] = dot(ext_t[CHAN : CHAN + 32, 0:ATOMS], hot[0:ATOMS, :])
    entry = lax.broadcasted_iota(jnp.int32, (8, GHOST), 1)
    axis = lax.broadcasted_iota(jnp.int32, (8, GHOST), 0)
    block = lax.div(entry, LIST)
    first = jnp.where(block < 3, -4.0, jnp.where(block > 4, 4.0, 0.0))
    left = (block == 0) | (block == 3) | (block == 5)
    right = (block == 2) | (block == 4) | (block == 7)
    second = jnp.where(left, -4.0, jnp.where(right, 4.0, 0.0))
    offset = jnp.where(axis == 0, first, jnp.where(axis == 1, second, 0.0))
    flags = jnp.concatenate([alive[i : i + 1, :] for i in range(SLOTS)], axis=1)
    centre = 1.0 + 0.75 * lax.broadcasted_iota(jnp.int32, (8, EDGES), 0).astype(F32)
    pick8[...] = jnp.concatenate([pick[...]] * 8, axis=0)

    for copy in copies1:
        copy.wait_recv()
    ghost_t = ext[ATOMS:ROWS, :].astype(F32).T
    ext_t[:, ATOMS:ROWS] = jnp.concatenate([ghost_t[0 : CHAN + 24], offset], axis=0).astype(LOW)

    found = near_found[...] + dot(ext_t[CHAN : CHAN + 32, ATOMS:ROWS], hot[ATOMS:ROWS, :])
    place = found[0:8] + found[8:16] + found[16:24] + found[24:32]
    unit[...] = place - jnp.concatenate([own_pos[...]] * SLOTS, axis=1)
    rel = [jnp.broadcast_to(unit[k : k + 1, :], (8, EDGES)) for k in range(3)]
    spread = jnp.sqrt(rel[0] * rel[0] + rel[1] * rel[1] + rel[2] * rel[2] + 1.0)
    inverse[...] = 1.0 / spread
    unit[...] = unit[...] * inverse[...]
    away = spread - centre
    basis = jnp.exp(-(away * away))
    slope[...] = -2.0 * away * basis
    blank = jnp.zeros((8, EDGES), F32)
    pre1 = dot(w1_t[...], jnp.concatenate([basis, blank], axis=0).astype(LOW))
    open1 = sigmoid(pre1)
    gate1[...] = pre1
    pre2 = dot(w2_t[...], (pre1 * open1).astype(LOW))
    open2 = sigmoid(pre2)
    gate2[...] = pre2
    hid2 = ((pre2 * open2).astype(LOW).astype(F32) * flags).astype(LOW)
    radial[...] = dot(w3_t[...], hid2)
    for i in range(SLOTS):
        tile = tile_of(i)
        toward = [-unit[k : k + 1, tile] for k in range(3)]
        for b in range(BANDS):
            own = proj_t[band(0, b), :]
            messages[band(0, b), tile] = (radial[band(0, b), tile] * own).astype(LOW)
            vector = radial[band(1, b), tile] * own
            for k in range(3):
                messages[band(k + 1, b), tile] = (vector * toward[k]).astype(LOW)

    send2[...] = dot(hot[ATOMS:ROWS, :], messages[...], NT).astype(LOW)
    copies2 = [
        push(1, j, send2.at[pl.ds(LIST * j, LIST), :], recv2.at[pl.ds(LIST * (7 - j), LIST), :])
        for j in range(8)
    ]
    for j in ORDER:
        copies2[j].start()

    partner[...] = dot(ext_t[0:CHAN, :], hot[...])
    agg[...] = dot(messages[...], hot[0:ATOMS, :], NT)
    for b in range(BANDS):
        total = [agg[band(k, b), :] for k in range(4)]
        for i in range(SLOTS):
            tile = tile_of(i)
            other = partner[band(0, b), tile]
            total[0] = total[0] + radial[band(0, b), tile] * other
            vector = radial[band(1, b), tile] * other
            for k in range(3):
                total[k + 1] = total[k + 1] + vector * unit[k : k + 1, tile]
        for k in range(4):
            agg[band(k, b), :] = total[k]
    rate = dot(w1_t[...], jnp.concatenate([slope[...], blank], axis=0).astype(LOW))
    rate = dot(w2_t[...], (rate * slope_of(gate1[...])).astype(LOW))
    rate = rate * slope_of(gate2[...]) * flags
    d_radial[...] = dot(w3_t[...], rate.astype(LOW))

    for copy in copies2:
        copy.wait_recv()
    back = recv2[0:LIST, :].astype(F32)
    for j in range(1, 8):
        back = back + recv2[LIST * j : LIST * (j + 1), :].astype(F32)
    agg[...] += dot(jnp.concatenate(split(back.T), axis=1), pick8[0 : 2 * LIST, :])

    along = [agg[(k + 1) * CHAN : (k + 2) * CHAN, :] for k in range(3)]
    norms = along[0] * along[0] + along[1] * along[1] + along[2] * along[2]
    lowered = jnp.concatenate([agg[0:CHAN, :].astype(LOW), norms.astype(LOW)], axis=0)
    pre = dot(fold_rows[...], lowered)
    pre = pre[0:16] + pre[16:32] + own_pre[...]
    opened = sigmoid(pre)
    energies_ref[...] = jnp.sum(pre * opened * out_weight[...], axis=0, keepdims=True)
    d_pre = out_weight[...] * opened * (1.0 + pre * (1.0 - opened))
    d_pre = d_pre.astype(LOW)
    back = dot(fold_columns[...], jnp.concatenate([d_pre, d_pre], axis=0))
    cot[0:CHAN, :] = back[0:CHAN].astype(LOW)
    d_norms = 2.0 * back[CHAN : 2 * CHAN]
    for k in range(3):
        cot[(k + 1) * CHAN : (k + 2) * CHAN, :] = (along[k] * d_norms).astype(LOW)
    send3[...] = dot(pick[...], cot[...], NT).astype(LOW)
    copies3 = [push(2, j, send3, recv3.at[pl.ds(LIST * (7 - j), LIST), :]) for j in range(8)]
    for j in ORDER:
        copies3[j].start()

    partner_cot[...] = dot(cot[...], hot[0:ATOMS, :])
    own_cot[...] = cot[...].astype(F32)
    for i in range(SLOTS):
        tile = tile_of(i)
        toward = [unit[k : k + 1, tile] for k in range(3)]
        sums = [jnp.zeros((8, ATOMS), F32) for k in range(4)]
        for b in range(BANDS):
            own = proj_t[band(0, b), :]
            other = partner[band(0, b), tile]
            weight = radial[band(1, b), tile]
            rate_s = d_radial[band(0, b), tile]
            rate_v = d_radial[band(1, b), tile]
            term = other * own_cot[band(0, b), :] + own * partner_cot[band(0, b), tile]
            spread_part = rate_s * term
            flow = jnp.zeros((BAND, ATOMS), F32)
            for k in range(3):
                term = other * own_cot[band(k + 1, b), :] - own * partner_cot[band(k + 1, b), tile]
                flow = flow + toward[k] * term
                sums[k + 1] = sums[k + 1] + fold(weight * term)
            sums[0] = sums[0] + fold(spread_part + rate_v * flow)
            factors[band(0, b), tile] = rate_s * own
            factors[band(1, b), tile] = rate_v * own
            factors[band(2, b), tile] = weight * own
        for k in range(4):
            partial[8 * k : 8 * k + 8, tile] = sums[k]

    for copy in copies3:
        copy.wait_recv()
    wide = CHAN // 4
    ghost_cot = recv3[...].astype(F32).T
    stacks = [
        jnp.concatenate(
            [ghost_cot[k * CHAN + h * wide : k * CHAN + (h + 1) * wide] for k in range(4)], axis=0
        ).astype(LOW)
        for h in range(4)
    ]
    for c in range(EDGES // 256):
        lanes = pl.ds(c * 256, 256)
        toward = [unit[k : k + 1, lanes] for k in range(3)]
        sums = [partial[8 * k : 8 * k + 8, lanes] for k in range(4)]
        for h in range(4):
            far = dot(stacks[h], hot[ATOMS:ROWS, lanes])
            rows = [pl.ds(k * CHAN + h * wide, wide) for k in range(3)]
            weight = factors[rows[2], lanes]
            flow = toward[0] * far[wide : 2 * wide]
            for k in range(1, 3):
                flow = flow + toward[k] * far[(k + 1) * wide : (k + 2) * wide]
            for k in range(3):
                sums[k + 1] = sums[k + 1] - fold(weight * far[(k + 1) * wide : (k + 2) * wide])
            spread_part = factors[rows[0], lanes] * far[0:wide]
            sums[0] = sums[0] + fold(spread_part - factors[rows[1], lanes] * flow)
        for k in range(4):
            partial[8 * k : 8 * k + 8, lanes] = sums[k]
    high, low = split(partial[...])
    halves = jnp.concatenate([high, low], axis=0)
    row = lax.broadcasted_iota(jnp.int32, (32, 64), 0)
    across = lax.broadcasted_iota(jnp.int32, (32, 64), 1)
    same = lax.div(row, 8) == lax.rem(lax.div(across, 8), 4)
    whole = dot(jnp.where(same, 1.0, 0.0).astype(LOW), halves)
    along = [unit[k : k + 1, :] for k in range(3)]
    lengthwise = whole[8:16] * along[0] + whole[16:24] * along[1] + whole[24:32] * along[2]
    place_row = lax.broadcasted_iota(jnp.int32, (8, EDGES), 0)
    pull = jnp.where(place_row == 2, whole[24:32], 0.0)
    pull = jnp.where(place_row == 1, whole[16:24], pull)
    pull = jnp.where(place_row == 0, whole[8:16], pull)
    change = (pull - unit[...] * lengthwise) * inverse[...] + unit[...] * whole[0:8]
    high, low = split(change)
    d_rel = jnp.concatenate([high.astype(F32), low.astype(F32)], axis=0).astype(LOW)

    parted = dot(d_rel, hot[ATOMS:ROWS, :], NT)
    send4[...] = parted[0:8] + parted[8:16]
    copies4 = [push(3, j, send4, recv4.at[7 - j]) for j in range(8)]
    for j in ORDER:
        copies4[j].start()
    near = dot(d_rel, hot[0:ATOMS, :], NT)
    force = -(near[0:8] + near[8:16])
    for i in range(SLOTS):
        force = force + change[:, i * ATOMS : (i + 1) * ATOMS]
    for copy in copies4:
        copy.wait_recv()
    lane_block = lax.div(lax.broadcasted_iota(jnp.int32, (8, GHOST), 1), LIST)
    back = recv4[0]
    for j in range(1, 8):
        back = jnp.where(lane_block == 7 - j, recv4[j], back)
    high, low = split(back)
    given = jnp.concatenate([high.astype(F32), low.astype(F32)], axis=0).astype(LOW)
    given = dot(given, pick8[...])
    force = force - (given[0:8] + given[8:16])
    forces_ref[...] = force[0:3]
    for copy in copies1 + copies2 + copies3 + copies4:
        copy.wait_send()


def body(
    n_dom,
    n_slab,
    features,
    positions,
    neighbours,
    neighbour_mask,
    ghost_list,
    w_up,
    radial_weight_1,
    radial_weight_2,
    radial_weight_3,
    w_a,
    w_b,
    w_o1,
    w_o2,
):
    operands = (
        features,
        positions,
        neighbours,
        neighbour_mask,
        ghost_list.reshape(1, LIST),
        w_up,
        radial_weight_1,
        radial_weight_2,
        radial_weight_3,
        w_a,
        w_b,
        w_o1.T,
        w_o2.reshape(1, 16),
    )
    operands = tuple(pltpu.with_memory_space_constraint(x, pltpu.HBM) for x in operands)
    held = [pltpu.VMEM(x.shape, x.dtype) for x in operands]
    energies, forces = pl.pallas_call(
        functools.partial(kernel, n_dom, n_slab),
        out_shape=(
            pltpu.VMEM((1, ATOMS), F32),
            pltpu.VMEM((3, ATOMS), F32),
        ),
        in_specs=[pl.BlockSpec(memory_space=pltpu.HBM)] * len(operands),
        out_specs=(
            pl.BlockSpec(memory_space=pltpu.VMEM),
            pl.BlockSpec(memory_space=pltpu.VMEM),
        ),
        scratch_shapes=held
        + [
            pltpu.VMEM((ROWS, 2 * CHAN), LOW),
            pltpu.VMEM((CHAN + 32, ROWS), LOW),
            pltpu.VMEM((8, ATOMS), F32),
            pltpu.VMEM((LIST, ATOMS), LOW),
            pltpu.VMEM((GHOST, ATOMS), LOW),
            pltpu.VMEM((SLOTS, ATOMS), F32),
            pltpu.VMEM((ROWS, EDGES), LOW),
            pltpu.VMEM((HIDDEN, 16), LOW),
            pltpu.VMEM((HIDDEN, HIDDEN), LOW),
            pltpu.VMEM((2 * CHAN, HIDDEN), LOW),
            pltpu.VMEM((32, 2 * CHAN), LOW),
            pltpu.VMEM((2 * CHAN, 32), LOW),
            pltpu.VMEM((16, ATOMS), F32),
            pltpu.VMEM((16, 1), F32),
            pltpu.VMEM((CHAN, ATOMS), F32),
            pltpu.VMEM((32, EDGES), F32),
            pltpu.VMEM((CHAN, EDGES), F32),
            pltpu.VMEM((8, EDGES), F32),
            pltpu.VMEM((8, EDGES), F32),
            pltpu.VMEM((8, EDGES), F32),
            pltpu.VMEM((HIDDEN, EDGES), F32),
            pltpu.VMEM((HIDDEN, EDGES), F32),
            pltpu.VMEM((2 * CHAN, EDGES), F32),
            pltpu.VMEM((2 * CHAN, EDGES), F32),
            pltpu.VMEM((4 * CHAN, EDGES), LOW),
            pltpu.VMEM((4 * CHAN, ATOMS), F32),
            pltpu.VMEM((4 * CHAN, ATOMS), LOW),
            pltpu.VMEM((4 * CHAN, ATOMS), F32),
            pltpu.VMEM((4 * CHAN, EDGES), F32),
            pltpu.VMEM((3 * CHAN, EDGES), F32),
            pltpu.VMEM((32, EDGES), F32),
            pltpu.VMEM((LIST, 2 * CHAN), LOW),
            pltpu.VMEM((GHOST, 4 * CHAN), LOW),
            pltpu.VMEM((GHOST, 4 * CHAN), LOW),
            pltpu.VMEM((LIST, 4 * CHAN), LOW),
            pltpu.VMEM((GHOST, 4 * CHAN), LOW),
            pltpu.VMEM((8, GHOST), F32),
            pltpu.VMEM((8, 8, GHOST), F32),
            pltpu.SemaphoreType.DMA((13,)),
            pltpu.SemaphoreType.DMA((4, 8)),
            pltpu.SemaphoreType.DMA((4, 8)),
        ],
        compiler_params=pltpu.CompilerParams(
            collective_id=0, has_side_effects=True, vmem_limit_bytes=48 * 1024 * 1024
        ),
    )(*operands)
    return energies.reshape(ATOMS), forces


def solution(mesh):
    split_rows = P(("dom", "slab"), None)
    split_lanes = P(None, ("dom", "slab"))
    split_flat = P(("dom", "slab"))
    in_specs = (split_rows, split_lanes, split_lanes, split_lanes, split_flat) + (P(),) * 8
    return jax.shard_map(
        functools.partial(body, mesh.shape["dom"], mesh.shape["slab"]),
        mesh=mesh,
        in_specs=in_specs,
        out_specs=(split_flat, split_lanes),
        check_vma=False,
    )
```
